128 devices in a mesh: group: 8 (over z, core), member: 16 (over y, x).
Axes of the slice: x: 4, y: 4, z: 4, core: 2. Of those that a mesh axis runs over, the one named last changes fastest.
Arguments:
- hist_row: int32 [128, 256], P(('group', 'member')), may hold values from 0 to 2047
- hist_owner: int32 [128, 256, 1], P(('group', 'member')), may hold values from 0 to 127; in each aligned block of 256 rows (0 to 255, 256 to 511, ..., all dimensions but the last counted through in order) at most 6 rows name the same one
- seq_len: int32 [128], P(('group', 'member')), may hold values from 128 to 256, as said below
- item_table: bfloat16 [262144, 512], P(('group', 'member')), may hold values from -6 to 6
- neg_rows: int32 [8, 8192], P('group', 'member'), may hold values from 0 to 2047
- in_weight: bfloat16 [512, 2048], replicated, may hold values from -0.25 to 0.25
- out_weight: bfloat16 [512, 512], replicated, may hold values from -0.25 to 0.25
Outputs:
- user_loss: float32 [128], P(('group', 'member'))
- in_grad: float32 [512, 2048], replicated
- out_grad: float32 [512, 512], replicated
- table_grad: float32 [262144, 512], P(('group', 'member'))
The draws below stay inside these ranges and needn't reach their ends.
Inputs may be any that keep to these rules, and one draw needn't show every extreme that they name: `hist_owner`: no owner is named by more than 6 events of one user's history, a bound that some history reaches. `seq_len`: positions from a user's length on are padding; some user has the full length.
All inputs are finite; a program needn't handle non-finite values.
Results may differ from the reference program's by a relative error of at most 0.019.
Values may be sent and summed in bfloat16 or wider, within the bound.
No kernel may reach another device: no remote copies, remote signals or barrier semaphores. Data moves between devices by JAX's collectives and lax.ppermute only.
A program may use at most 128 MiB of HBM per device.

```python
import math
import jax
import jax.numpy as jnp
import numpy as np
from jax import lax

D = 512
HEADS = 4
LEN = 256
NEG_DEV = 512
ROWS_OWN = 2048
NEG = 8192
USERS = 128
ITEMS = 262144
CAP = 6
N_GROUP = 8
N_MEMBER = 16
DEVICES = 128


def draw_seq_len(key, part):
    key = jax.random.fold_in(key, 7)
    lengths = jax.random.randint(key, (USERS,), LEN // 2, LEN + 1, dtype=jnp.int32)
    return lengths.at[0].set(LEN)


def set_ends(array, own_key, least, largest):
    longest = array.shape.index(max(array.shape))
    spots = []
    for shift in (0, 1):
        where = [jax.random.randint(jax.random.fold_in(own_key, axis), (), 0, length) for axis, length in enumerate(array.shape)]
        where[longest] = (where[longest] + shift) % array.shape[longest]
        spots.append(tuple(where))
    return array.at[spots[0]].set(least).at[spots[1]].set(largest)


def level_of(rng, dims, pieces, smallest, largest):
    level, own = 1.0, jax.random.fold_in(rng, 6)
    for dim, blocks in pieces:
        heights = jnp.exp(jax.random.uniform(jax.random.fold_in(own, dim), (blocks,), jnp.float32, smallest / len(pieces), largest / len(pieces)))
        level = level * jnp.repeat(heights, dims[dim] // blocks).reshape([-1 if axis == dim else 1 for axis in range(len(dims))])
    return level


def rank_table(count, slope):
    portions = [(1 << 20) // math.isqrt(rank ** slope) + 1 for rank in range(1, count + 1)]
    scale = 1 + sum(portions) // (1 << 30)
    return np.cumsum(np.array([max(1, weight // scale) for weight in portions]))


def skewed_ids(own_key, dims, number_of, slope):
    table = rank_table(number_of, slope)
    ticket = jax.random.randint(jax.random.fold_in(own_key, 1), dims, 0, int(table[number_of - 1]))
    rank = jnp.searchsorted(jnp.asarray(table, jnp.int32), ticket, side="right")
    return jax.random.permutation(jax.random.fold_in(own_key, 2), number_of)[rank].astype(jnp.int32)


def deal_out(stream_key, own, number, rows, count, top, limit, lean):
    order = jax.random.permutation(stream_key, count)
    crowded, usual = load_shares(count, rows * top, limit, lean, True), load_shares(count, rows * top, limit, lean, False)
    places = jnp.arange(count)

    def named(sizes, turn):
        used = int((sizes > 0).sum())
        fixed = max(1, used // 4)
        moved = fixed + (places - fixed + turn * (used - fixed)) % max(1, count - fixed)
        return jnp.zeros((count,), jnp.int32).at[order[jnp.where(places < fixed, places, moved)]].set(jnp.asarray(sizes, jnp.int32))

    sizes = jnp.where(number % 4 == 0, named(crowded, number // 4), named(usual, number - number // 4 - 1))
    mixed = jax.random.permutation(jax.random.fold_in(own, 3), count)
    source_of, receiver = mixed[0:count // 2 * 2:2], mixed[1:count // 2 * 2:2]
    room = jnp.minimum(sizes[source_of] - 1, limit - sizes[receiver]) // 2
    room = jnp.where((source_of == order[0]) | (receiver == order[0]) | (sizes[receiver] == 0), 0, jnp.maximum(room, 0))
    moved = jax.random.randint(jax.random.fold_in(own, 4), (count // 2,), 0, 1 << 20) % (room + 1)
    sizes = sizes.at[source_of].add(-moved).at[receiver].add(moved)
    labels = jnp.searchsorted(jnp.cumsum(sizes), jnp.arange(rows * top), side="right").astype(jnp.int32)
    listing = labels.reshape(top, rows).T
    listing = listing[jax.random.permutation(jax.random.fold_in(own, 1), rows)]
    turn = jax.random.randint(jax.random.fold_in(own, 2), (rows, 1), 0, top)
    return jnp.take_along_axis(listing, (jnp.arange(top)[None, :] + turn) % top, axis=1)


def load_shares(number_of, total, limit, slope, full):
    weights = [(1 << 20) // math.isqrt(standing ** slope) + 1 for standing in range(1, number_of + 1)]
    largest = limit if full else min(limit, max(-(-total // number_of), total * weights[0] // sum(weights)))
    least = 1 if total - largest >= number_of - 1 else 0
    given, spare = [largest] + [least] * (number_of - 1), total - largest - least * (number_of - 1)
    while spare > 0:
        free = [i for i in range(1, number_of) if given[i] < largest] or [i for i in range(1, number_of) if given[i] < limit]
        whole, remaining = sum([weights[i] for i in free]), spare
        for i in free:
            addition = min(limit - given[i], max(1, remaining * weights[i] // whole), spare)
            given[i] = given[i] + addition
            spare = spare - addition
    return np.array(given)


def noise(rng, extent, width, limit, cuts=(), held_as=jnp.bfloat16):
    values = jax.random.normal(rng, extent, jnp.float32) * width
    if len(cuts) > 0:
        values = level_of(rng, extent, cuts, -0.22, 0.18) * values
    return jnp.clip(values, min=-limit, max=limit).astype(held_as)


def setup_inputs(seed: int = 0) -> dict:
    streams_of = jax.random.split(jax.random.key(seed), 8)
    hist_row = set_ends(skewed_ids(streams_of[0], (USERS, LEN), ROWS_OWN, 2), jax.random.fold_in(streams_of[0], 3), 0, ROWS_OWN - 1).astype(jnp.int32)
    hist_owner_keys = jax.random.split(jax.random.fold_in(streams_of[1], 1), USERS * LEN // LEN)
    hist_owner_turns = jax.random.permutation(jax.random.fold_in(streams_of[1], 3), USERS * LEN // LEN)
    hist_owner = jax.vmap(lambda own, number: deal_out(jax.random.fold_in(streams_of[1], 2), own, number, LEN, DEVICES, 1, CAP, 2))(hist_owner_keys, hist_owner_turns).reshape((USERS, LEN, 1))
    seq_len = draw_seq_len(jax.random.fold_in(streams_of[7], 71), 0)
    item_table = noise(streams_of[3], (ITEMS, D), 1.0, 6.0, ((0, 128),))
    neg_rows = set_ends(jax.random.randint(streams_of[4], (N_GROUP, NEG), 0, ROWS_OWN), jax.random.fold_in(streams_of[4], 1), 0, ROWS_OWN - 1).astype(jnp.int32)
    in_weight = noise(streams_of[5], (D, 4 * D), D ** -0.5, 0.25)
    out_weight = noise(streams_of[6], (D, D), D ** -0.5, 0.25)
    return {"hist_row": hist_row, "hist_owner": hist_owner, "seq_len": seq_len, "item_table": item_table, "neg_rows": neg_rows, "in_weight": in_weight, "out_weight": out_weight}


inverse_temp = 20.0

def layer_norm(values):
    average = lax.optimization_barrier(jnp.mean(values, axis=-1, keepdims=True))
    centered = values - average
    return centered * lax.rsqrt(lax.optimization_barrier(jnp.mean(centered * centered, axis=-1, keepdims=True)) + 1e-05)

def hstu_layer(history, in_wide, out_wide, length):
    seqlen, model_width = history.shape
    head_size = model_width // HEADS
    normed = layer_norm(history).astype(jnp.bfloat16)
    hidden = jax.nn.silu(jnp.dot(normed, in_wide.astype(jnp.bfloat16), preferred_element_type=jnp.float32)).astype(jnp.bfloat16)
    gate_cols = hidden[:, :model_width]
    value_cols = hidden[:, model_width:2 * model_width].reshape(seqlen, HEADS, head_size)
    query_cols = hidden[:, 2 * model_width:3 * model_width].reshape(seqlen, HEADS, head_size)
    key_cols = hidden[:, 3 * model_width:].reshape(seqlen, HEADS, head_size)
    scores = jnp.einsum('qhd,khd->hqk', query_cols.astype(jnp.float32), key_cols.astype(jnp.float32)) * head_size ** (-0.5)
    position = jnp.arange(seqlen)
    allowed = (position[None, :] <= position[:, None]) & (position[None, :] < length)
    attention = (jax.nn.silu(scores) * allowed[None].astype(jnp.float32) / length.astype(jnp.float32)).astype(jnp.bfloat16)
    mixed_heads = jnp.einsum('hqk,khd->qhd', attention.astype(jnp.float32), value_cols.astype(jnp.float32)).reshape(seqlen, model_width)
    gated_out = (layer_norm(mixed_heads) * gate_cols.astype(jnp.float32)).astype(jnp.bfloat16)
    return jnp.dot(gated_out, out_wide.astype(jnp.bfloat16), preferred_element_type=jnp.float32) + history

def sampled_loss(output, history, negatives, length):
    seqlen = output.shape[0]
    query_scale = lax.rsqrt(lax.optimization_barrier(jnp.sum(output * output, axis=-1, keepdims=True)) + 1e-06)
    query_unit = output * query_scale
    query_bf = query_unit.astype(jnp.bfloat16)
    following = jnp.concatenate([history[1:], jnp.zeros_like(history[:1])], axis=0)
    pos_scale = lax.rsqrt(lax.optimization_barrier(jnp.sum(following * following, axis=-1, keepdims=True)) + 1e-06)
    pos_unit = following * pos_scale
    pos_score = inverse_temp * lax.optimization_barrier(jnp.sum(query_unit * pos_unit, axis=-1))
    neg_score = inverse_temp * lax.dot_general(query_bf, negatives, (((1,), (1,)), ((), ())), preferred_element_type=jnp.float32)
    log_total = jnp.log(jnp.exp(pos_score) + lax.optimization_barrier(jnp.sum(jnp.exp(neg_score), axis=-1)))
    usable = (jnp.arange(seqlen) < length - 1).astype(jnp.float32)
    user_loss = jnp.sum((log_total - pos_score) * usable) / (length - 1).astype(jnp.float32)
    pos_grad = inverse_temp * usable * (jnp.exp(pos_score - log_total) - 1.0)
    neg_weight = (inverse_temp * usable[:, None] * jnp.exp(neg_score - log_total[:, None])).astype(jnp.bfloat16)
    query_grad = pos_grad[:, None] * pos_unit + jnp.dot(neg_weight, negatives, preferred_element_type=jnp.float32)
    output_grad = query_scale * (query_grad - query_unit * lax.optimization_barrier(jnp.sum(query_unit * query_grad, axis=-1, keepdims=True)))
    unit_grad = pos_grad[:, None] * query_unit
    next_grad = pos_scale * (unit_grad - pos_unit * lax.optimization_barrier(jnp.sum(pos_unit * unit_grad, axis=-1, keepdims=True)))
    shifted = jnp.concatenate([jnp.zeros_like(next_grad[:1]), next_grad[:-1]], axis=0)
    neg_sum = lax.dot_general(neg_weight, query_bf, (((0,), (0,)), ((), ())), preferred_element_type=jnp.float32)
    return (user_loss, output_grad, shifted, neg_sum)

def reference(hist_row, hist_owner, seq_len, item_table, neg_rows, in_weight, out_weight):
    model_width = item_table.shape[1]
    item_ids = (hist_owner[:, :, 0] * ROWS_OWN + hist_row).astype(jnp.int32)
    column = jnp.arange(NEG) // NEG_DEV
    neg_ids = ((jnp.arange(N_GROUP)[:, None] * N_MEMBER + column[None, :]) * ROWS_OWN + neg_rows).astype(jnp.int32)
    neg_full = item_table[neg_ids].astype(jnp.float32)
    neg_scale = lax.rsqrt(lax.optimization_barrier(jnp.sum(neg_full * neg_full, axis=-1, keepdims=True)) + 1e-06)
    neg_unit = neg_full * neg_scale
    neg_bf = neg_unit.astype(jnp.bfloat16)
    in_wide = in_weight.astype(jnp.float32)
    out_wide = out_weight.astype(jnp.float32)

    def user_step(running, user_index):
        neg_accum, in_accum, out_accum = running
        group_index = user_index // N_MEMBER
        history = item_table[item_ids[user_index]].astype(jnp.float32)
        length = seq_len[user_index]
        output, pullback = jax.vjp(lambda first, second, third: hstu_layer(first, second, third, length), history, in_wide, out_wide)
        user_loss, output_grad, shifted, neg_sum = sampled_loss(output, history, neg_bf[group_index], length)
        history_grad, in_part, out_part = pullback(output_grad)
        running = (neg_accum.at[group_index].add(neg_sum), in_accum + in_part, out_accum + out_part)
        return (running, (user_loss, history_grad + shifted))
    starting = (jnp.zeros((N_GROUP, NEG, model_width), jnp.float32), jnp.zeros(in_wide.shape, jnp.float32), jnp.zeros(out_wide.shape, jnp.float32))
    running, (losses, row_grad) = lax.scan(user_step, starting, jnp.arange(USERS))
    neg_accum, in_grad, out_grad = running
    neg_grad = neg_scale * (neg_accum - neg_unit * lax.optimization_barrier(jnp.sum(neg_unit * neg_accum, axis=-1, keepdims=True)))
    table_grad = jnp.zeros((ITEMS, model_width), jnp.float32)
    table_grad = table_grad.at[item_ids.reshape(-1)].add(row_grad.reshape(-1, model_width))
    table_grad = table_grad.at[neg_ids.reshape(-1)].add(neg_grad.reshape(-1, model_width))
    return (losses, in_grad, out_grad, table_grad)
```

```python
import functools
import jax
import jax.numpy as jnp
from jax import lax
from jax.experimental import pallas as pl
from jax.experimental.pallas import tpu as pltpu
from jax.sharding import PartitionSpec as P

HEADS = 4
SLOTS = 8
SIDE = 4
TEMP = 20.0
BF = jnp.bfloat16
F32 = jnp.float32
AXES = ("group", "member")
MIB = 1024 * 1024


def mm(a, b):
    return jnp.dot(a, b, preferred_element_type=F32)


def mm_nt(a, b):
    return lax.dot_general(a, b, (((1,), (1,)), ((), ())), preferred_element_type=F32)


def mm_tn(a, b):
    return lax.dot_general(a, b, (((0,), (0,)), ((), ())), preferred_element_type=F32)


def iota(shape, dim):
    return lax.broadcasted_iota(jnp.int32, shape, dim)


def ones_where(mask):
    return jnp.where(mask, 1.0, 0.0).astype(BF)


def sigmoid(v):
    return 0.5 * jnp.tanh(0.5 * v) + 0.5


def norm_parts(values):
    centered = values - jnp.mean(values, axis=-1, keepdims=True)
    scale = lax.rsqrt(jnp.mean(centered * centered, axis=-1, keepdims=True) + 1e-05)
    return centered * scale, scale


def norm_back(unit, scale, grad):
    return scale * (
        grad
        - jnp.mean(grad, axis=-1, keepdims=True)
        - unit * jnp.mean(grad * unit, axis=-1, keepdims=True)
    )


def row_to_col(row):
    size = row.shape[1]
    eye = iota((128, 128), 0) == iota((128, 128), 1)
    parts = [
        jnp.sum(jnp.where(eye, row[:, k : k + 128], 0), axis=1, keepdims=True)
        for k in range(0, size, 128)
    ]
    return jnp.concatenate(parts, axis=0)


def col_to_rows(col):
    return jnp.transpose(jnp.broadcast_to(col, (col.shape[0], 128)))[:8]


class Fetched:
    def __init__(self, source, here, sem):
        self.here, self.shape, self.waited = here, here.shape, False
        self.copy = pltpu.make_async_copy(source, here, sem)
        self.copy.start()

    def __getitem__(self, index):
        if not self.waited:
            self.copy.wait()
            self.waited = True
        return self.here[index]


class Sent:
    def __init__(self, target, here, sems):
        self.target, self.here, self.sems, self.copies = target, here, sems, []
        self.shape, self.dtype = here.shape, here.dtype

    def __getitem__(self, index):
        return self.here[index]

    def __setitem__(self, index, value):
        self.here[index] = value
        if index is Ellipsis:
            source, target = self.here, self.target
        else:
            source, target = self.here.at[index], self.target.at[index]
        copy = pltpu.make_async_copy(source, target, self.sems.at[len(self.copies)])
        copy.start()
        self.copies.append(copy)


PARTS = 8
FAR = False


def call(
    kernel, outs, *args, smem=(), far=(), far_out=(), flops=0, name=None, scratch=(), after=(), vmem=40
):
    if not FAR:
        far, far_out = (), ()
    in_specs = [
        pl.BlockSpec(memory_space=pltpu.SMEM if i in smem else pl.ANY if i in far else pltpu.VMEM)
        for i in range(len(args))
    ] + [pl.BlockSpec(memory_space=pl.ANY)] * len(after)
    given, late, shown = len(args), len(after), len(outs)
    hidden = [pltpu.VMEM(args[i].shape, args[i].dtype) for i in far]
    hidden += [pltpu.VMEM(outs[i].shape, outs[i].dtype) for i in far_out]
    hidden += [pltpu.SemaphoreType.DMA((len(far) + 1,))]
    hidden += [pltpu.SemaphoreType.DMA((PARTS,)) for _ in far_out]

    def body(*refs):
        ins, results = list(refs[:given]), list(refs[given + late : given + late + shown])
        rest = refs[given + late + shown :]
        own, rest = rest[: len(scratch)], rest[len(scratch) :]
        sems = rest[len(far) + len(far_out)]
        for n, i in enumerate(far):
            ins[i] = Fetched(ins[i], rest[n], sems.at[n])
        sent = []
        for n, i in enumerate(far_out):
            results[i] = Sent(results[i], rest[len(far) + n], rest[len(far) + len(far_out) + 1 + n])
            sent.append(results[i])
        kernel(*ins, *results, *own)
        for result in sent:
            for copy in result.copies:
                copy.wait()

    moved = sum(a.size * a.dtype.itemsize for a in args)
    moved += sum(o.size * o.dtype.itemsize for o in outs)
    return pl.pallas_call(
        body,
        out_shape=outs,
        in_specs=in_specs,
        out_specs=[
            pl.BlockSpec(memory_space=pltpu.HBM if i in far_out else pltpu.VMEM)
            for i in range(len(outs))
        ],
        scratch_shapes=list(scratch) + hidden,
        compiler_params=pltpu.CompilerParams(vmem_limit_bytes=vmem * MIB),
        cost_estimate=pl.CostEstimate(flops=flops, bytes_accessed=moved, transcendentals=0),
        name=name,
    )(*args, *after)


def out(shape, dtype):
    return jax.ShapeDtypeStruct(shape, dtype)


def slots_kernel(owner_ref, row_ref, slots_ref, req_ref):
    owner = row_to_col(owner_ref[...])
    seqlen = owner.shape[0]
    devices = req_ref.shape[0]
    named = ones_where(owner == iota((seqlen, devices), 1))
    earlier = ones_where(iota((seqlen, seqlen), 0) > iota((seqlen, seqlen), 1))
    before = mm(earlier, named)
    place = jnp.sum(before * named.astype(F32), axis=1, keepdims=True).astype(jnp.int32)
    slots_ref[...] = owner * SLOTS + place
    wanted = row_to_col(row_ref[...])
    at_place = iota((seqlen, 128), 1) == place
    high = jnp.where(at_place, wanted >> 6, 0).astype(F32).astype(BF)
    low = jnp.where(at_place, wanted & 63, 0).astype(F32).astype(BF)
    asked = mm_tn(named, high) * 64.0 + mm_tn(named, low)
    req_ref[...] = asked[:, :SLOTS].astype(jnp.int32)


def find_kernel(asked_ref, table_ref, found_ref):
    asked = asked_ref[...]
    devices = asked.shape[0]
    rows = table_ref.shape[0]
    block = 256
    high = (asked >> 6).astype(F32).astype(BF)
    low = (asked & 63).astype(F32).astype(BF)
    for k in range(0, devices * SLOTS, block):
        spread = ones_where(
            (iota((block, devices), 0) + k) // SLOTS == iota((block, devices), 1)
        )
        every = mm(spread, high) * 64.0 + mm(spread, low)
        mine = (iota((block, SLOTS), 0) & (SLOTS - 1)) == iota((block, SLOTS), 1)
        ids = jnp.sum(jnp.where(mine, every, 0.0), axis=1, keepdims=True).astype(jnp.int32)
        pick = ones_where(ids == iota((block, rows), 1))
        found_ref[k : k + block, :] = mm(pick, table_ref[...]).astype(BF)


def own_kernel(ids_ref, table_ref, rows_ref, unit_ref):
    ids = row_to_col(ids_ref[...])
    rows = table_ref.shape[0]
    block = 256
    for k in range(0, ids.shape[0], block):
        pick = ones_where(ids[k : k + block] == iota((block, rows), 1))
        got = mm(pick, table_ref[...])
        rows_ref[k : k + block, :] = got.astype(BF)
        scale = lax.rsqrt(jnp.sum(got * got, axis=-1, keepdims=True) + 1e-06)
        unit_ref[k : k + block, :] = (got * scale).astype(BF)


def attention_of(query, key, length):
    seqlen, head_size = query.shape
    scores = mm_nt(query, key) * head_size ** (-0.5)
    at, of = iota((seqlen, seqlen), 0), iota((seqlen, seqlen), 1)
    allowed = (of <= at) & (of < length)
    share = jnp.where(allowed, 1.0 / length.astype(F32), 0.0)
    return scores, share


def following_of(history):
    seqlen = history.shape[0]
    moved = pltpu.roll(history, seqlen - 1, 0)
    return jnp.where(iota(history.shape, 0) < seqlen - 1, moved, 0.0)


def layer(length, history, in_ref, out_ref, mixed_ref, pre_ref=None):
    width = history.shape[1]
    head = width // HEADS
    normed = norm_parts(history.astype(F32))[0].astype(BF)
    parts = []
    for k in range(4):
        pre = mm(normed, in_ref[:, k * width : (k + 1) * width])
        if pre_ref is not None:
            pre_ref[:, k * width : (k + 1) * width] = pre
        parts.append((pre * sigmoid(pre)).astype(BF))
    gate, values, queries, keys = parts
    for h in range(HEADS):
        cols = slice(h * head, (h + 1) * head)
        scores, share = attention_of(queries[:, cols], keys[:, cols], length)
        attention = (scores * sigmoid(scores) * share).astype(BF)
        mixed_ref[:, cols] = mm(attention, values[:, cols])
    gated = (norm_parts(mixed_ref[...])[0] * gate.astype(F32)).astype(BF)
    return mm(gated, out_ref[...]) + history.astype(F32)


def forward_kernel(
    len_ref, back_ref, slots_ref, in_ref, out_ref, hist_ref, query_ref, pos_ref, mixed_ref
):
    seqlen = hist_ref.shape[0]
    length = len_ref[0]
    pick = ones_where(slots_ref[...] == iota((seqlen, back_ref.shape[0]), 1))
    hist_ref[...] = mm(pick, back_ref[...]).astype(BF)
    output = layer(length, hist_ref[...], in_ref, out_ref, mixed_ref)
    scale = lax.rsqrt(jnp.sum(output * output, axis=-1, keepdims=True) + 1e-06)
    query_unit = output * scale
    query_ref[...] = query_unit.astype(BF)
    following = following_of(hist_ref[...].astype(F32))
    pos_scale = lax.rsqrt(jnp.sum(following * following, axis=-1, keepdims=True) + 1e-06)
    pos_score = TEMP * jnp.sum(query_unit * (following * pos_scale), axis=-1, keepdims=True)
    rows = col_to_rows(pos_score)
    usable = jnp.where(iota(rows.shape, 1) < length - 1, 1.0, 0.0)
    pos_ref[...] = jnp.where(iota(rows.shape, 0) == 0, rows, usable)


def again_kernel(len_ref, hist_ref, in_ref, out_ref, pre_ref, mixed_ref, output_ref):
    output_ref[...] = layer(len_ref[0], hist_ref[...], in_ref, out_ref, mixed_ref, pre_ref)


def scores_kernel(count, query_ref, *refs):
    negs, others = refs[:SIDE], refs[SIDE : SIDE + count]
    weights_ref, grad_ref, total_ref = refs[-3:]
    query = query_ref[...]
    total = jnp.zeros((query.shape[0], 1), F32)
    grad = jnp.zeros(query.shape, F32)
    for k, neg_ref in enumerate(negs):
        neg = neg_ref[...]
        size = neg.shape[0]
        weight = jnp.exp(TEMP * mm_nt(query, neg))
        total = total + jnp.sum(weight, axis=1, keepdims=True)
        weight = weight.astype(BF)
        weights_ref[:, k * size : (k + 1) * size] = weight
        grad = grad + mm(weight, neg)
    grad_ref[...] = grad.astype(grad_ref.dtype)
    total = col_to_rows(total)
    row = iota(total.shape, 0)
    for k, ref in enumerate(others[:-1]):
        total = jnp.where(row == k, ref[...], total)
    if others:
        total = jnp.where(row == SIDE, others[-1][0:1, :], total)
        total = jnp.where(row == SIDE + 1, others[-1][1:2, :], total)
    total_ref[...] = total


def row_to_f32_col(row):
    return jnp.transpose(jnp.broadcast_to(row, (128, row.shape[1])))[:, 0:1]


def neg_kernel(len_ref, *refs):
    packs, queries, weights = refs[:SIDE], refs[SIDE : 2 * SIDE], refs[2 * SIDE : 3 * SIDE]
    outs, (loss_ref, factor_ref) = refs[3 * SIDE : -2], refs[-2:]
    scaled = []
    for k, query_ref in enumerate(queries):
        pos_score, usable = packs[k][SIDE : SIDE + 1, :], packs[k][SIDE + 1 : SIDE + 2, :]
        total = jnp.exp(pos_score)
        for j, ref in enumerate(packs):
            total = total + ref[j ^ k : (j ^ k) + 1, :]
        log_total = jnp.log(total)
        if k == 0:
            loss = jnp.sum((log_total - pos_score) * usable, axis=1, keepdims=True)
            loss_ref[...] = loss / (len_ref[0] - 1).astype(F32)
        factor = row_to_f32_col(TEMP * usable * jnp.exp(-log_total))
        if k == 0:
            factor_ref[...] = factor
        scaled.append((query_ref[...].astype(F32) * factor).astype(BF))
    for k, ref in enumerate(outs):
        size = ref.shape[0]
        cols = slice(k * size, (k + 1) * size)
        total = mm_tn(weights[0][:, cols], scaled[0])
        for w, q in zip(weights[1:], scaled[1:]):
            total = total + mm_tn(w[:, cols], q)
        ref[...] = total.astype(ref.dtype)


def backward_kernel(
    len_ref, at_ref, factor_ref, sum0, sum1, sum2, sum3, hist_ref, pre_ref, mixed_ref, output_ref,
    in_ref, out_ref,
    row_ref, keep_ref, send_ref,
    normed_ref, gated_ref, dpre_ref,
):
    length = len_ref[0]
    core = at_ref[3]
    seqlen, width = hist_ref.shape
    head = width // HEADS
    history = hist_ref[...].astype(F32)
    output = output_ref[...]
    query_scale = lax.rsqrt(jnp.sum(output * output, axis=-1, keepdims=True) + 1e-06)
    query_unit = output * query_scale
    following = following_of(history)
    pos_scale = lax.rsqrt(jnp.sum(following * following, axis=-1, keepdims=True) + 1e-06)
    pos_unit = following * pos_scale
    pos_score = TEMP * jnp.sum(query_unit * pos_unit, axis=-1, keepdims=True)
    from_negs = jnp.zeros((seqlen, width), F32)
    for ref in (sum0, sum1, sum2, sum3):
        from_negs = from_negs + ref[...].astype(F32)
    usable = jnp.where(iota((seqlen, 1), 0) < length - 1, 1.0, 0.0)
    factor = factor_ref[...]
    pos_grad = factor * jnp.exp(pos_score) - TEMP * usable
    query_grad = pos_grad * pos_unit + factor * from_negs
    output_grad = query_scale * (
        query_grad - query_unit * jnp.sum(query_unit * query_grad, axis=-1, keepdims=True)
    )
    unit_grad = pos_grad * query_unit
    next_grad = pos_scale * (
        unit_grad - pos_unit * jnp.sum(pos_unit * unit_grad, axis=-1, keepdims=True)
    )
    shifted = jnp.where(iota((seqlen, width), 0) > 0, pltpu.roll(next_grad, 1, 0), 0.0)

    def hidden_of(k):
        pre = pre_ref[:, k * width : (k + 1) * width]
        return (pre * sigmoid(pre)).astype(BF)

    def store(k, cols, grad):
        cols = slice(k * width + cols.start, k * width + cols.stop)
        pre = pre_ref[:, cols]
        s = sigmoid(pre)
        grad = grad.astype(BF).astype(F32) * (s * (1.0 + pre * (1.0 - s)))
        dpre_ref[:, cols] = grad.astype(BF)

    gate = hidden_of(0).astype(F32)
    mixed_unit, mixed_scale = norm_parts(mixed_ref[...])
    gated_ref[...] = (mixed_unit * gate).astype(BF)
    output_bf = output_grad.astype(BF)
    d_gated = mm_nt(output_bf, out_ref[...]).astype(BF).astype(F32)
    store(0, slice(0, width), d_gated * mixed_unit)
    d_mixed = norm_back(mixed_unit, mixed_scale, d_gated * gate).astype(BF)
    values, queries, keys = hidden_of(1), hidden_of(2), hidden_of(3)
    for h in range(HEADS):
        cols = slice(h * head, (h + 1) * head)
        q, k, v, d = queries[:, cols], keys[:, cols], values[:, cols], d_mixed[:, cols]
        scores, share = attention_of(q, k, length)
        s = sigmoid(scores)
        attention = (scores * s * share).astype(BF)
        d_attention = mm_nt(d, v).astype(BF).astype(F32)
        d_scores = d_attention * share * (s * (1.0 + scores * (1.0 - s)))
        d_scores = (d_scores * head ** (-0.5)).astype(BF)
        store(1, cols, mm_tn(attention, d))
        store(2, cols, mm(d_scores, k))
        store(3, cols, mm_tn(d_scores, q))
    normed, scale = norm_parts(history)
    normed_ref[...] = normed.astype(BF)
    half = width // 2
    for ref, which in ((send_ref, 1 - core), (keep_ref, core)):
        rows = pl.ds(pl.multiple_of(which * half, half), half)
        mine = normed_ref[:, rows]
        for k in range(4):
            cols = slice(k * width, (k + 1) * width)
            ref[:, cols] = mm_tn(mine, dpre_ref[:, cols]).astype(BF)
        ref[:, 4 * width :] = mm_tn(gated_ref[:, rows], output_bf).astype(BF)
    d_normed = mm_nt(dpre_ref[...], in_ref[...]).astype(BF).astype(F32)
    row_ref[...] = (output_grad + norm_back(normed, scale, d_normed) + shifted).astype(BF)


def going_kernel(slots_ref, row_ref, going_ref):
    pick = ones_where(slots_ref[...] == iota((row_ref.shape[0], going_ref.shape[0]), 1))
    going_ref[...] = mm_tn(pick, row_ref[...]).astype(BF)


def table_kernel(
    asked_ref, arrived_ref, ids_ref, rows_ref, neg0, neg1, neg2, neg3, table_ref, grad_ref
):
    block = table_ref.shape[0]

    @pl.when(pl.program_id(0) == 0)
    def _():
        rows = rows_ref[...].astype(F32)
        scale = lax.rsqrt(jnp.sum(rows * rows, axis=-1, keepdims=True) + 1e-06)
        unit = rows * scale
        total = neg0[...] + neg1[...].astype(F32) + neg2[...].astype(F32) + neg3[...].astype(F32)
        grad = scale * (total - unit * jnp.sum(unit * total, axis=-1, keepdims=True))
        grad_ref[...] = grad.astype(BF)

    first = pl.program_id(0) * block
    asked, ids = asked_ref[...], ids_ref[...]
    pick = ones_where(asked == iota((block, asked.shape[1]), 0) + first)
    total = mm(pick, arrived_ref[...])
    pick = ones_where(ids == iota((block, ids.shape[1]), 0) + first)
    table_ref[...] = total + mm(pick, grad_ref[...])


def table_grad_of(asked, arrived, ids, rows, negs, owned):
    width = arrived.shape[1]
    block = 512
    whole = pl.BlockSpec(memory_space=pltpu.VMEM)
    return pl.pallas_call(
        table_kernel,
        grid=(owned // block,),
        out_shape=out((owned, width), F32),
        in_specs=[whole] * 8,
        out_specs=pl.BlockSpec((block, width), lambda i: (i, 0)),
        scratch_shapes=[pltpu.VMEM(rows.shape, BF)],
        compiler_params=pltpu.CompilerParams(vmem_limit_bytes=40 * MIB),
        cost_estimate=pl.CostEstimate(
            flops=2 * owned * (arrived.shape[0] + rows.shape[0]) * width,
            bytes_accessed=owned * width * 4,
            transcendentals=0,
        ),
        name="table_grad",
    )(asked, arrived, ids, rows, *negs)


def quarters(at_ref, place, total_ref, outs):
    me = at_ref[place]
    for s, ref in enumerate(outs):
        size = ref.shape[0]
        which = (me + s) & (SIDE - 1)
        part = total_ref[pl.ds(pl.multiple_of(which * size, size), size), :]
        ref[...] = part.astype(ref.dtype)


def sum_of(refs):
    total = refs[0][...].astype(F32)
    for ref in refs[1:]:
        total = total + ref[...].astype(F32)
    return total


def scatter_kernel(place, count, at_ref, *refs):
    ins, outs, total_ref = refs[:count], refs[count:-1], refs[-1]
    total_ref[...] = sum_of(ins)
    quarters(at_ref, place, total_ref, outs)


def last_kernel(*refs):
    refs[-1][...] = sum_of(refs[:-1]).astype(refs[-1].dtype)


def total_kernel(p0, p1, p2, p3, total_ref):
    even = p0[...].astype(F32) + p2[...].astype(F32)
    odd = p1[...].astype(F32) + p3[...].astype(F32)
    total_ref[...] = (even + odd).astype(total_ref.dtype)


def stack_kernel(*refs):
    size = refs[0].shape[0]
    for k, ref in enumerate(refs[:-1]):
        refs[-1][k * size : (k + 1) * size] = ref[...]


def place_kernel(at_ref, mine_ref, other_ref, in_ref, out_ref):
    y, z, core = at_ref[1], at_ref[2], at_ref[3]
    count, rows, cols = mine_ref.shape
    half, width = in_ref.shape[0] // 2, in_ref.shape[1]
    for which, ref in ((core, mine_ref), (1 - core, other_ref)):
        for i in range(count):
            row = which * half + ((z - i // SIDE) & 3) * (half // SIDE)
            row = row + ((y - i % SIDE) & 3) * rows
            place = pl.ds(pl.multiple_of(row, rows), rows)
            part = ref[i].astype(F32)
            in_ref[place, :] = part[:, :width]
            out_ref[place, :] = part[:, width:]


def moves(axis, shift):
    if axis == "z":
        return "group", [(z * 2 + c, (z + shift) % SIDE * 2 + c) for z in range(SIDE) for c in range(2)]
    if axis == "core":
        return "group", [(g, g ^ 1) for g in range(2 * SIDE)]
    pairs = [(y, x) for y in range(SIDE) for x in range(SIDE)]
    if axis == "x":
        return "member", [(y * SIDE + x, y * SIDE + (x + shift) % SIDE) for y, x in pairs]
    return "member", [(y * SIDE + x, (y + shift) % SIDE * SIDE + x) for y, x in pairs]


def shift_by(value, axis, shift):
    name, pairs = moves(axis, shift)
    return lax.ppermute(value, name, pairs)


def spread(value, axis):
    return [value] + [shift_by(value, axis, s) for s in range(1, SIDE)]


def across(value, kind):
    step = 1 if kind == "queries" else 3
    masks = (step, step * SIDE, step * SIDE + step)
    return [
        lax.ppermute(v, "member", [(m, m ^ mask) for m in range(SIDE * SIDE)])
        for v, mask in zip(value, masks)
    ]


def scatter(at, place, ins, after=()):
    rows, cols = ins[0].shape
    piece = (rows // SIDE, cols)
    return call(
        functools.partial(scatter_kernel, place, len(ins)),
        [out(piece, F32)] + [out(piece, BF)] * (SIDE - 1),
        at,
        *ins,
        smem=(0,),
        scratch=[pltpu.VMEM((rows, cols), F32)],
        after=after,
        name="scatter",
    )


def exchanged(parts, axis):
    return [parts[0]] + [shift_by(parts[s], axis, s) for s in range(1, SIDE)]


def reduced(at, parts, after_z, after_x):
    parts = scatter(at, 1, parts, after_z)
    (piece,) = call(last_kernel, [out(parts[0].shape, BF)], *exchanged(parts, "y"), name="last")
    (piece,) = call(
        total_kernel, [out(piece.shape, BF)], *spread(piece, "x"), after=after_x, name="total"
    )
    return piece


def gathered(at, piece, after):
    rows, cols = piece.shape
    width = rows * 2 * SIDE * SIDE
    piece = jnp.concatenate(spread(piece[None], "y"), axis=0)
    (piece,) = call(
        stack_kernel,
        [out((SIDE * SIDE, rows, cols), BF)],
        *spread(piece, "z"),
        after=after,
        name="stack",
    )
    return call(
        place_kernel,
        [out((width, cols - width), F32), out((width, width), F32)],
        at,
        piece,
        shift_by(piece, "core", 1),
        smem=(0,),
        name="place",
    )


def local(hist_row, hist_owner, seq_len, item_table, neg_rows, in_weight, out_weight):
    devices = lax.axis_size(AXES)
    seqlen = hist_row.shape[1]
    owned, width = item_table.shape
    count = neg_rows.shape[1]
    group, member = lax.axis_index("group"), lax.axis_index("member")
    at = jnp.stack([member % SIDE, member // SIDE, group // 2, group % 2]).astype(jnp.int32)

    own_rows, own_bf = call(
        own_kernel,
        [out((count, width), BF), out((count, width), BF)],
        neg_rows,
        item_table,
        flops=2 * count * owned * width,
        name="own_negatives",
    )
    negs = [own_bf] + across([own_bf] * 3, "negatives")
    slots, requests = call(
        slots_kernel,
        [out((seqlen, 1), jnp.int32), out((devices, SLOTS), jnp.int32)],
        hist_owner.reshape(1, seqlen),
        hist_row,
        after=(own_bf,),
        name="slots",
    )
    asked = lax.all_to_all(requests, AXES, split_axis=0, concat_axis=0, tiled=True)
    (found,) = call(
        find_kernel,
        [out((devices * SLOTS, width), BF)],
        asked,
        item_table,
        flops=2 * devices * SLOTS * owned * width,
        after=(negs[1], negs[2]),
        name="find_rows",
    )
    back = lax.all_to_all(
        found.reshape(devices, SLOTS, width), AXES, split_axis=0, concat_axis=0, tiled=True
    ).reshape(devices * SLOTS, width)
    history, query, pos = call(
        forward_kernel,
        [out((seqlen, width), BF), out((seqlen, width), BF), out((8, seqlen), F32)],
        seq_len,
        back,
        slots,
        in_weight,
        out_weight,
        smem=(0,),
        scratch=[pltpu.VMEM((seqlen, width), F32)],
        flops=2 * seqlen * width * (devices * SLOTS + 6 * width),
        name="forward",
    )
    queries = [query] + across([query] * 3, "queries")
    weights, sums, totals = [], [], []
    for s, q in enumerate(queries):
        others = (*totals, pos) if s == SIDE - 1 else ()
        w, total, pack = call(
            functools.partial(scores_kernel, len(others)),
            [
                out((seqlen, SIDE * count), BF),
                out((seqlen, width), F32 if s == 0 else BF),
                out((8, seqlen), F32),
            ],
            q,
            *negs,
            *others,
            flops=4 * seqlen * SIDE * count * width,
            after=sums[:1],
            name="scores",
        )
        weights.append(w)
        sums.append(total)
        totals.append(pack)
    sums[1:] = across(sums[1:], "queries")
    packs = [pack] + across([pack] * 3, "queries")
    pre, mixed, output = call(
        again_kernel,
        [out((seqlen, 4 * width), F32), out((seqlen, width), F32), out((seqlen, width), F32)],
        seq_len,
        history,
        in_weight,
        out_weight,
        smem=(0,),
        flops=2 * seqlen * width * 6 * width,
        after=(pack,),
        name="layer_again",
    )
    *neg_parts, loss, factor = call(
        neg_kernel,
        [out((count, width), F32)]
        + [out((count, width), BF)] * (SIDE - 1)
        + [out((1, 1), F32), out((seqlen, 1), F32)],
        seq_len,
        *packs,
        *queries,
        *weights,
        smem=(0,),
        flops=2 * SIDE * seqlen * SIDE * count * width,
        after=(output,),
        name="negative_sums",
    )
    sent = across(neg_parts[1:], "negatives")
    row_grad, keep, send = call(
        backward_kernel,
        [
            out((seqlen, width), BF),
            out((width // 2, 5 * width), BF),
            out((width // 2, 5 * width), BF),
        ],
        seq_len,
        at,
        factor,
        *sums,
        history,
        pre,
        mixed,
        output,
        in_weight,
        out_weight,
        smem=(0, 1),
        scratch=[
            pltpu.VMEM((seqlen, width), BF),
            pltpu.VMEM((seqlen, width), BF),
            pltpu.VMEM((seqlen, 4 * width), BF),
        ],
        flops=2 * seqlen * width * 14 * width,
        name="backward",
    )
    got = shift_by(send, "core", 1)
    z_parts = exchanged(scatter(at, 2, [keep, got]), "z")
    (going,) = call(
        going_kernel,
        [out((devices * SLOTS, width), BF)],
        slots,
        row_grad,
        flops=2 * devices * SLOTS * seqlen * width,
        name="going",
    )
    arrived = lax.all_to_all(
        going.reshape(devices, SLOTS, width), AXES, split_axis=0, concat_axis=0, tiled=True
    ).reshape(devices * SLOTS, width)
    piece = reduced(at, z_parts, (*sent,), (arrived,))
    table_grad = table_grad_of(
        asked.reshape(1, devices * SLOTS), arrived, neg_rows, own_rows, [neg_parts[0], *sent], owned
    )
    in_grad, out_grad = gathered(at, piece, (table_grad,))
    return (loss.reshape(1), in_grad, out_grad, table_grad)


def solution(mesh):
    return jax.shard_map(
        local,
        mesh=mesh,
        in_specs=(
            P(AXES, None),
            P(AXES, None, None),
            P(AXES),
            P(AXES, None),
            P("group", "member"),
            P(),
            P(),
        ),
        out_specs=(P(AXES), P(), P(), P(AXES, None)),
        check_vma=False,
    )
```

```python
import functools
import jax
import jax.numpy as jnp
from jax import lax
from jax.experimental import pallas as pl
from jax.experimental.pallas import tpu as pltpu
from jax.sharding import PartitionSpec as P

HEADS = 4
SLOTS = 8
SIDE = 4
TEMP = 20.0
BF = jnp.bfloat16
F32 = jnp.float32
AXES = ("group", "member")
MIB = 1024 * 1024


def mm(a, b):
    return jnp.dot(a, b, preferred_element_type=F32)


def mm_nt(a, b):
    return lax.dot_general(a, b, (((1,), (1,)), ((), ())), preferred_element_type=F32)


def mm_tn(a, b):
    return lax.dot_general(a, b, (((0,), (0,)), ((), ())), preferred_element_type=F32)


def iota(shape, dim):
    return lax.broadcasted_iota(jnp.int32, shape, dim)


def ones_where(mask):
    return jnp.where(mask, 1.0, 0.0).astype(BF)


def sigmoid(v):
    return 0.5 * jnp.tanh(0.5 * v) + 0.5


def norm_parts(values):
    centered = values - jnp.mean(values, axis=-1, keepdims=True)
    scale = lax.rsqrt(jnp.mean(centered * centered, axis=-1, keepdims=True) + 1e-05)
    return centered * scale, scale


def norm_back(unit, scale, grad):
    return scale * (
        grad
        - jnp.mean(grad, axis=-1, keepdims=True)
        - unit * jnp.mean(grad * unit, axis=-1, keepdims=True)
    )


def row_to_col(row):
    size = row.shape[1]
    eye = iota((128, 128), 0) == iota((128, 128), 1)
    parts = [
        jnp.sum(jnp.where(eye, row[:, k : k + 128], 0), axis=1, keepdims=True)
        for k in range(0, size, 128)
    ]
    return jnp.concatenate(parts, axis=0)


def col_to_rows(col):
    return jnp.transpose(jnp.broadcast_to(col, (col.shape[0], 128)))[:8]


class Fetched:
    def __init__(self, source, here, sem):
        self.here, self.shape, self.waited = here, here.shape, False
        self.copy = pltpu.make_async_copy(source, here, sem)
        self.copy.start()

    def __getitem__(self, index):
        if not self.waited:
            self.copy.wait()
            self.waited = True
        return self.here[index]


class Sent:
    def __init__(self, target, here, sems):
        self.target, self.here, self.sems, self.copies = target, here, sems, []
        self.shape, self.dtype = here.shape, here.dtype

    def __getitem__(self, index):
        return self.here[index]

    def __setitem__(self, index, value):
        self.here[index] = value
        if index is Ellipsis:
            source, target = self.here, self.target
        else:
            source, target = self.here.at[index], self.target.at[index]
        copy = pltpu.make_async_copy(source, target, self.sems.at[len(self.copies)])
        copy.start()
        self.copies.append(copy)


PARTS = 8
FAR = False


def call(
    kernel, outs, *args, smem=(), far=(), far_out=(), flops=0, name=None, scratch=(), after=(), vmem=40
):
    if not FAR:
        far, far_out = (), ()
    in_specs = [
        pl.BlockSpec(memory_space=pltpu.SMEM if i in smem else pl.ANY if i in far else pltpu.VMEM)
        for i in range(len(args))
    ] + [pl.BlockSpec(memory_space=pl.ANY)] * len(after)
    given, late, shown = len(args), len(after), len(outs)
    hidden = [pltpu.VMEM(args[i].shape, args[i].dtype) for i in far]
    hidden += [pltpu.VMEM(outs[i].shape, outs[i].dtype) for i in far_out]
    hidden += [pltpu.SemaphoreType.DMA((len(far) + 1,))]
    hidden += [pltpu.SemaphoreType.DMA((PARTS,)) for _ in far_out]

    def body(*refs):
        ins, results = list(refs[:given]), list(refs[given + late : given + late + shown])
        rest = refs[given + late + shown :]
        own, rest = rest[: len(scratch)], rest[len(scratch) :]
        sems = rest[len(far) + len(far_out)]
        for n, i in enumerate(far):
            ins[i] = Fetched(ins[i], rest[n], sems.at[n])
        sent = []
        for n, i in enumerate(far_out):
            results[i] = Sent(results[i], rest[len(far) + n], rest[len(far) + len(far_out) + 1 + n])
            sent.append(results[i])
        kernel(*ins, *results, *own)
        for result in sent:
            for copy in result.copies:
                copy.wait()

    moved = sum(a.size * a.dtype.itemsize for a in args)
    moved += sum(o.size * o.dtype.itemsize for o in outs)
    return pl.pallas_call(
        body,
        out_shape=outs,
        in_specs=in_specs,
        out_specs=[
            pl.BlockSpec(memory_space=pltpu.HBM if i in far_out else pltpu.VMEM)
            for i in range(len(outs))
        ],
        scratch_shapes=list(scratch) + hidden,
        compiler_params=pltpu.CompilerParams(vmem_limit_bytes=vmem * MIB),
        cost_estimate=pl.CostEstimate(flops=flops, bytes_accessed=moved, transcendentals=0),
        name=name,
    )(*args, *after)


def out(shape, dtype):
    return jax.ShapeDtypeStruct(shape, dtype)


def later(values, after):
    count = len(values)
    anywhere = pl.BlockSpec(memory_space=pl.ANY)
    return pl.pallas_call(
        lambda *refs: None,
        out_shape=[out(v.shape, v.dtype) for v in values],
        in_specs=[anywhere] * (count + len(after)),
        out_specs=[anywhere] * count,
        input_output_aliases={i: i for i in range(count)},
        cost_estimate=pl.CostEstimate(flops=0, bytes_accessed=0, transcendentals=0),
        name="later",
    )(*values, *after)


def slots_kernel(owner_ref, row_ref, slots_ref, req_ref):
    owner = row_to_col(owner_ref[...])
    seqlen = owner.shape[0]
    devices = req_ref.shape[0]
    named = ones_where(owner == iota((seqlen, devices), 1))
    earlier = ones_where(iota((seqlen, seqlen), 0) > iota((seqlen, seqlen), 1))
    before = mm(earlier, named)
    place = jnp.sum(before * named.astype(F32), axis=1, keepdims=True).astype(jnp.int32)
    slots_ref[...] = owner * SLOTS + place
    wanted = row_to_col(row_ref[...])
    at_place = iota((seqlen, 128), 1) == place
    high = jnp.where(at_place, wanted >> 6, 0).astype(F32).astype(BF)
    low = jnp.where(at_place, wanted & 63, 0).astype(F32).astype(BF)
    asked = mm_tn(named, high) * 64.0 + mm_tn(named, low)
    req_ref[...] = asked[:, :SLOTS].astype(jnp.int32)


def find_kernel(asked_ref, table_ref, found_ref):
    asked = asked_ref[...]
    devices = asked.shape[0]
    rows = table_ref.shape[0]
    block = 256
    high = (asked >> 6).astype(F32).astype(BF)
    low = (asked & 63).astype(F32).astype(BF)
    for k in range(0, devices * SLOTS, block):
        spread = ones_where(
            (iota((block, devices), 0) + k) // SLOTS == iota((block, devices), 1)
        )
        every = mm(spread, high) * 64.0 + mm(spread, low)
        mine = (iota((block, SLOTS), 0) & (SLOTS - 1)) == iota((block, SLOTS), 1)
        ids = jnp.sum(jnp.where(mine, every, 0.0), axis=1, keepdims=True).astype(jnp.int32)
        pick = ones_where(ids == iota((block, rows), 1))
        found_ref[k : k + block, :] = mm(pick, table_ref[...]).astype(BF)


def own_kernel(ids_ref, table_ref, rows_ref, unit_ref):
    ids = row_to_col(ids_ref[...])
    rows = table_ref.shape[0]
    block = 256
    for k in range(0, ids.shape[0], block):
        pick = ones_where(ids[k : k + block] == iota((block, rows), 1))
        got = mm(pick, table_ref[...])
        rows_ref[k : k + block, :] = got.astype(BF)
        scale = lax.rsqrt(jnp.sum(got * got, axis=-1, keepdims=True) + 1e-06)
        unit_ref[k : k + block, :] = (got * scale).astype(BF)


def attention_of(query, key, length):
    seqlen, head_size = query.shape
    scores = mm_nt(query, key) * head_size ** (-0.5)
    at, of = iota((seqlen, seqlen), 0), iota((seqlen, seqlen), 1)
    allowed = (of <= at) & (of < length)
    share = jnp.where(allowed, 1.0 / length.astype(F32), 0.0)
    return scores, share


def following_of(history):
    seqlen = history.shape[0]
    moved = pltpu.roll(history, seqlen - 1, 0)
    return jnp.where(iota(history.shape, 0) < seqlen - 1, moved, 0.0)


def layer(length, history, in_ref, out_ref, mixed_ref, pre_ref=None):
    width = history.shape[1]
    head = width // HEADS
    normed = norm_parts(history.astype(F32))[0].astype(BF)
    parts = []
    for k in range(4):
        pre = mm(normed, in_ref[:, k * width : (k + 1) * width])
        if pre_ref is not None:
            pre_ref[:, k * width : (k + 1) * width] = pre
        parts.append((pre * sigmoid(pre)).astype(BF))
    gate, values, queries, keys = parts
    for h in range(HEADS):
        cols = slice(h * head, (h + 1) * head)
        scores, share = attention_of(queries[:, cols], keys[:, cols], length)
        attention = (scores * sigmoid(scores) * share).astype(BF)
        mixed_ref[:, cols] = mm(attention, values[:, cols])
    gated = (norm_parts(mixed_ref[...])[0] * gate.astype(F32)).astype(BF)
    return mm(gated, out_ref[...]) + history.astype(F32)


def forward_kernel(
    len_ref, back_ref, slots_ref, in_ref, out_ref, hist_ref, query_ref, pos_ref, mixed_ref
):
    seqlen = hist_ref.shape[0]
    length = len_ref[0]
    pick = ones_where(slots_ref[...] == iota((seqlen, back_ref.shape[0]), 1))
    hist_ref[...] = mm(pick, back_ref[...]).astype(BF)
    output = layer(length, hist_ref[...], in_ref, out_ref, mixed_ref)
    scale = lax.rsqrt(jnp.sum(output * output, axis=-1, keepdims=True) + 1e-06)
    query_unit = output * scale
    query_ref[...] = query_unit.astype(BF)
    following = following_of(hist_ref[...].astype(F32))
    pos_scale = lax.rsqrt(jnp.sum(following * following, axis=-1, keepdims=True) + 1e-06)
    pos_score = TEMP * jnp.sum(query_unit * (following * pos_scale), axis=-1, keepdims=True)
    rows = col_to_rows(pos_score)
    usable = jnp.where(iota(rows.shape, 1) < length - 1, 1.0, 0.0)
    pos_ref[...] = jnp.where(iota(rows.shape, 0) == 0, rows, usable)


def again_kernel(
    len_ref, hist_ref, in_ref, out_ref, pre_ref, mixed_ref, output_ref
):
    output_ref[...] = layer(len_ref[0], hist_ref[...], in_ref, out_ref, mixed_ref, pre_ref)


def scores_kernel(query_ref, *refs):
    negs, others, (weights_ref, grad_ref, total_ref) = refs[:SIDE], refs[SIDE:-3], refs[-3:]
    query = query_ref[...]
    total = jnp.zeros((query.shape[0], 1), F32)
    grad = jnp.zeros(query.shape, F32)
    for k, neg_ref in enumerate(negs):
        neg = neg_ref[...]
        size = neg.shape[0]
        weight = jnp.exp(TEMP * mm_nt(query, neg))
        total = total + jnp.sum(weight, axis=1, keepdims=True)
        weight = weight.astype(BF)
        weights_ref[:, k * size : (k + 1) * size] = weight
        grad = grad + mm(weight, neg)
    grad_ref[...] = grad.astype(grad_ref.dtype)
    total = col_to_rows(total)
    row = iota(total.shape, 0)
    for k, ref in enumerate(others[:-1]):
        total = jnp.where(row == k, ref[...], total)
    if others:
        total = jnp.where(row == SIDE, others[-1][0:1, :], total)
        total = jnp.where(row == SIDE + 1, others[-1][1:2, :], total)
    total_ref[...] = total


def row_to_f32_col(row):
    return jnp.transpose(jnp.broadcast_to(row, (128, row.shape[1])))[:, 0:1]


def neg_kernel(len_ref, *refs):
    packs, queries, weights = refs[:SIDE], refs[SIDE : 2 * SIDE], refs[2 * SIDE : 3 * SIDE]
    own_ref, first_ref, second_ref, third_ref, last_ref, loss_ref, factor_ref = refs[3 * SIDE :]
    half = own_ref.shape[1] // 2
    scaled = []
    for k, query_ref in enumerate(queries):
        pos_score, usable = packs[k][SIDE : SIDE + 1, :], packs[k][SIDE + 1 : SIDE + 2, :]
        total = jnp.exp(pos_score)
        for j, ref in enumerate(packs):
            total = total + ref[j ^ k : (j ^ k) + 1, :]
        log_total = jnp.log(total)
        if k == 0:
            loss = jnp.sum((log_total - pos_score) * usable, axis=1, keepdims=True)
            loss_ref[...] = loss / (len_ref[0] - 1).astype(F32)
        factor = row_to_f32_col(TEMP * usable * jnp.exp(-log_total))
        if k == 0:
            factor_ref[...] = factor
        scaled.append((query_ref[...].astype(F32) * factor).astype(BF))
    for k in range(SIDE):
        size = own_ref.shape[0]
        cols = slice(k * size, (k + 1) * size)
        total = mm_tn(weights[0][:, cols], scaled[0])
        for w, q in zip(weights[1:], scaled[1:]):
            total = total + mm_tn(w[:, cols], q)
        left, right = total[:, :half].astype(BF), total[:, half:].astype(BF)
        if k == 0:
            own_ref[...] = total
        elif k == 1:
            first_ref[0], last_ref[...] = left, right
        elif k == 2:
            third_ref[...], second_ref[0] = left, right
        else:
            first_ref[1], second_ref[1] = left, right


def turn_kernel(third_ref, from_first, last_ref, from_second, over_third, over_last):
    third = third_ref[...].astype(F32) + from_first[1].astype(F32)
    over_third[...] = third.astype(BF)
    last = last_ref[...].astype(F32) + from_second[1].astype(F32)
    over_last[...] = last.astype(BF)


def backward_kernel(
    len_ref, at_ref, factor_ref, sum0, sum1, sum2, sum3, hist_ref, pre_ref, mixed_ref, output_ref,
    in_ref, out_ref,
    row_ref, keep_ref, send_ref,
    normed_ref, gated_ref, dpre_ref,
):
    length = len_ref[0]
    core = at_ref[3]
    seqlen, width = hist_ref.shape
    head = width // HEADS
    history = hist_ref[...].astype(F32)
    output = output_ref[...]
    query_scale = lax.rsqrt(jnp.sum(output * output, axis=-1, keepdims=True) + 1e-06)
    query_unit = output * query_scale
    following = following_of(history)
    pos_scale = lax.rsqrt(jnp.sum(following * following, axis=-1, keepdims=True) + 1e-06)
    pos_unit = following * pos_scale
    pos_score = TEMP * jnp.sum(query_unit * pos_unit, axis=-1, keepdims=True)
    from_negs = jnp.zeros((seqlen, width), F32)
    for ref in (sum0, sum1, sum2, sum3):
        from_negs = from_negs + ref[...].astype(F32)
    usable = jnp.where(iota((seqlen, 1), 0) < length - 1, 1.0, 0.0)
    factor = factor_ref[...]
    pos_grad = factor * jnp.exp(pos_score) - TEMP * usable
    query_grad = pos_grad * pos_unit + factor * from_negs
    output_grad = query_scale * (
        query_grad - query_unit * jnp.sum(query_unit * query_grad, axis=-1, keepdims=True)
    )
    unit_grad = pos_grad * query_unit
    next_grad = pos_scale * (
        unit_grad - pos_unit * jnp.sum(pos_unit * unit_grad, axis=-1, keepdims=True)
    )
    shifted = jnp.where(iota((seqlen, width), 0) > 0, pltpu.roll(next_grad, 1, 0), 0.0)

    def hidden_of(k):
        pre = pre_ref[:, k * width : (k + 1) * width]
        return (pre * sigmoid(pre)).astype(BF)

    def store(k, cols, grad):
        cols = slice(k * width + cols.start, k * width + cols.stop)
        pre = pre_ref[:, cols]
        s = sigmoid(pre)
        grad = grad.astype(BF).astype(F32) * (s * (1.0 + pre * (1.0 - s)))
        dpre_ref[:, cols] = grad.astype(BF)

    gate = hidden_of(0).astype(F32)
    mixed_unit, mixed_scale = norm_parts(mixed_ref[...])
    gated_ref[...] = (mixed_unit * gate).astype(BF)
    output_bf = output_grad.astype(BF)
    d_gated = mm_nt(output_bf, out_ref[...]).astype(BF).astype(F32)
    store(0, slice(0, width), d_gated * mixed_unit)
    d_mixed = norm_back(mixed_unit, mixed_scale, d_gated * gate).astype(BF)
    values, queries, keys = hidden_of(1), hidden_of(2), hidden_of(3)
    for h in range(HEADS):
        cols = slice(h * head, (h + 1) * head)
        q, k, v, d = queries[:, cols], keys[:, cols], values[:, cols], d_mixed[:, cols]
        scores, share = attention_of(q, k, length)
        s = sigmoid(scores)
        attention = (scores * s * share).astype(BF)
        d_attention = mm_nt(d, v).astype(BF).astype(F32)
        d_scores = d_attention * share * (s * (1.0 + scores * (1.0 - s)))
        d_scores = (d_scores * head ** (-0.5)).astype(BF)
        store(1, cols, mm_tn(attention, d))
        store(2, cols, mm(d_scores, k))
        store(3, cols, mm_tn(d_scores, q))
    normed, scale = norm_parts(history)
    normed_ref[...] = normed.astype(BF)
    half = width // 2
    for ref, which in ((send_ref, 1 - core), (keep_ref, core)):
        rows = pl.ds(pl.multiple_of(which * half, half), half)
        mine = normed_ref[:, rows]
        for k in range(4):
            cols = slice(k * width, (k + 1) * width)
            ref[:, cols] = mm_tn(mine, dpre_ref[:, cols]).astype(BF)
        ref[:, 4 * width :] = mm_tn(gated_ref[:, rows], output_bf).astype(BF)
    d_normed = mm_nt(dpre_ref[...], in_ref[...]).astype(BF).astype(F32)
    row_ref[...] = (output_grad + norm_back(normed, scale, d_normed) + shifted).astype(BF)


def going_kernel(slots_ref, row_ref, going_ref):
    pick = ones_where(slots_ref[...] == iota((row_ref.shape[0], going_ref.shape[0]), 1))
    going_ref[...] = mm_tn(pick, row_ref[...]).astype(BF)


def table_kernel(
    asked_ref, arrived_ref, ids_ref, rows_ref, own_ref, first_ref, second_ref, third_ref, last_ref,
    table_ref, done_ref, grad_ref,
):
    block = table_ref.shape[0]

    @pl.when(pl.program_id(0) == 0)
    def _():
        rows = rows_ref[...].astype(F32)
        scale = lax.rsqrt(jnp.sum(rows * rows, axis=-1, keepdims=True) + 1e-06)
        unit = rows * scale
        left = first_ref[0].astype(F32) + third_ref[...].astype(F32)
        right = second_ref[0].astype(F32) + last_ref[...].astype(F32)
        total = own_ref[...] + jnp.concatenate([left, right], axis=1)
        grad = scale * (total - unit * jnp.sum(unit * total, axis=-1, keepdims=True))
        grad_ref[...] = grad.astype(BF)
        done_ref[...] = jnp.zeros(done_ref.shape, F32)

    first = pl.program_id(0) * block
    asked, ids = asked_ref[...], ids_ref[...]
    pick = ones_where(asked == iota((block, asked.shape[1]), 0) + first)
    total = mm(pick, arrived_ref[...])
    pick = ones_where(ids == iota((block, ids.shape[1]), 0) + first)
    table_ref[...] = total + mm(pick, grad_ref[...])


def table_grad_of(asked, arrived, ids, rows, negs, owned):
    width = arrived.shape[1]
    block = 512
    whole = pl.BlockSpec(memory_space=pltpu.VMEM)
    return pl.pallas_call(
        table_kernel,
        grid=(owned // block,),
        out_shape=[out((owned, width), F32), out((8, 128), F32)],
        in_specs=[whole] * 9,
        out_specs=[
            pl.BlockSpec((block, width), lambda i: (i, 0)),
            pl.BlockSpec((8, 128), lambda i: (0, 0)),
        ],
        scratch_shapes=[pltpu.VMEM(rows.shape, BF)],
        compiler_params=pltpu.CompilerParams(vmem_limit_bytes=40 * MIB),
        cost_estimate=pl.CostEstimate(
            flops=2 * owned * (arrived.shape[0] + rows.shape[0]) * width,
            bytes_accessed=owned * width * 4,
            transcendentals=0,
        ),
        name="table_grad",
    )(asked, arrived, ids, rows, *negs)


def quarters(at_ref, place, total_ref, outs):
    me = at_ref[place]
    for s, ref in enumerate(outs):
        size = ref.shape[0]
        which = (me + s) & (SIDE - 1)
        part = total_ref[pl.ds(pl.multiple_of(which * size, size), size), :]
        ref[...] = part.astype(ref.dtype)


def sum_of(refs):
    total = refs[0][...].astype(F32)
    for ref in refs[1:]:
        total = total + ref[...].astype(F32)
    return total


def scatter_kernel(place, count, at_ref, *refs):
    ins, outs, total_ref = refs[:count], refs[count:-1], refs[-1]
    total_ref[...] = sum_of(ins)
    quarters(at_ref, place, total_ref, outs)


def last_kernel(*refs):
    refs[-1][...] = sum_of(refs[:-1]).astype(refs[-1].dtype)


def total_kernel(p0, p1, p2, p3, total_ref):
    even = p0[...].astype(F32) + p2[...].astype(F32)
    odd = p1[...].astype(F32) + p3[...].astype(F32)
    total_ref[...] = (even + odd).astype(total_ref.dtype)


def stack_kernel(*refs):
    size = refs[0].shape[0]
    for k, ref in enumerate(refs[:-1]):
        refs[-1][k * size : (k + 1) * size] = ref[...]


def place_kernel(at_ref, mine_ref, other_ref, in_ref, out_ref):
    y, z, core = at_ref[1], at_ref[2], at_ref[3]
    count, rows, cols = mine_ref.shape
    half, width = in_ref.shape[0] // 2, in_ref.shape[1]
    for which, ref in ((core, mine_ref), (1 - core, other_ref)):
        for i in range(count):
            row = which * half + ((z - i // SIDE) & 3) * (half // SIDE)
            row = row + ((y - i % SIDE) & 3) * rows
            place = pl.ds(pl.multiple_of(row, rows), rows)
            part = ref[i].astype(F32)
            in_ref[place, :] = part[:, :width]
            out_ref[place, :] = part[:, width:]


def moves(axis, shift):
    if axis == "z":
        return "group", [(z * 2 + c, (z + shift) % SIDE * 2 + c) for z in range(SIDE) for c in range(2)]
    if axis == "core":
        return "group", [(g, g ^ 1) for g in range(2 * SIDE)]
    pairs = [(y, x) for y in range(SIDE) for x in range(SIDE)]
    if axis == "x":
        return "member", [(y * SIDE + x, y * SIDE + (x + shift) % SIDE) for y, x in pairs]
    return "member", [(y * SIDE + x, (y + shift) % SIDE * SIDE + x) for y, x in pairs]


def shift_by(value, axis, shift):
    name, pairs = moves(axis, shift)
    return lax.ppermute(value, name, pairs)


def spread(value, axis):
    return [value] + [shift_by(value, axis, s) for s in range(1, SIDE)]


def square(value, axis):
    step = 3 if axis == "x" else 3 * SIDE
    return lax.ppermute(value, "member", [(m, m ^ step) for m in range(SIDE * SIDE)])


def across(value, kind):
    step = 1 if kind == "queries" else 3
    masks = (step, step * SIDE, step * SIDE + step)
    return [
        lax.ppermute(v, "member", [(m, m ^ mask) for m in range(SIDE * SIDE)])
        for v, mask in zip(value, masks)
        if v is not None
    ]


def scatter(at, place, ins, after=()):
    rows, cols = ins[0].shape
    piece = (rows // SIDE, cols)
    return call(
        functools.partial(scatter_kernel, place, len(ins)),
        [out(piece, F32)] + [out(piece, BF)] * (SIDE - 1),
        at,
        *ins,
        smem=(0,),
        scratch=[pltpu.VMEM((rows, cols), F32)],
        after=after,
        name="scatter",
    )


def exchanged(parts, axis):
    return [parts[0]] + [shift_by(parts[s], axis, s) for s in range(1, SIDE)]


def reduced(parts, after):
    (piece,) = call(last_kernel, [out(parts[0].shape, BF)], *exchanged(parts, "y"), name="last")
    (piece,) = call(
        total_kernel, [out(piece.shape, BF)], *spread(piece, "x"), after=after, name="total"
    )
    return piece


def gathered(at, piece, after):
    rows, cols = piece.shape
    width = rows * 2 * SIDE * SIDE
    piece = jnp.concatenate(spread(piece[None], "y"), axis=0)
    (piece,) = call(
        stack_kernel,
        [out((SIDE * SIDE, rows, cols), BF)],
        *spread(piece, "z"),
        after=after,
        name="stack",
    )
    return call(
        place_kernel,
        [out((width, cols - width), F32), out((width, width), F32)],
        at,
        piece,
        shift_by(piece, "core", 1),
        smem=(0,),
        name="place",
    )


def local(hist_row, hist_owner, seq_len, item_table, neg_rows, in_weight, out_weight):
    devices = lax.axis_size(AXES)
    seqlen = hist_row.shape[1]
    owned, width = item_table.shape
    count = neg_rows.shape[1]
    group, member = lax.axis_index("group"), lax.axis_index("member")
    at = jnp.stack([member % SIDE, member // SIDE, group // 2, group % 2]).astype(jnp.int32)

    own_rows, own_bf = call(
        own_kernel,
        [out((count, width), BF), out((count, width), BF)],
        neg_rows,
        item_table,
        flops=2 * count * owned * width,
        name="own_negatives",
    )
    negs = [own_bf] + across([own_bf] * 3, "negatives")
    slots, requests = call(
        slots_kernel,
        [out((seqlen, 1), jnp.int32), out((devices, SLOTS), jnp.int32)],
        hist_owner.reshape(1, seqlen),
        hist_row,
        after=(own_bf,),
        name="slots",
    )
    asked = lax.all_to_all(requests, AXES, split_axis=0, concat_axis=0, tiled=True)
    (found,) = call(
        find_kernel,
        [out((devices * SLOTS, width), BF)],
        asked,
        item_table,
        flops=2 * devices * SLOTS * owned * width,
        after=(negs[1], negs[2]),
        name="find_rows",
    )
    back = lax.all_to_all(
        found.reshape(devices, SLOTS, width), AXES, split_axis=0, concat_axis=0, tiled=True
    ).reshape(devices * SLOTS, width)
    history, query, pos = call(
        forward_kernel,
        [out((seqlen, width), BF), out((seqlen, width), BF), out((8, seqlen), F32)],
        seq_len,
        back,
        slots,
        in_weight,
        out_weight,
        smem=(0,),
        scratch=[pltpu.VMEM((seqlen, width), F32)],
        flops=2 * seqlen * width * (devices * SLOTS + 6 * width),
        name="forward",
    )
    queries = [query] + across([query] * 3, "queries")
    weights, sums, totals = [], [], []
    for s, q in enumerate(queries):
        others = (*totals, pos) if s == SIDE - 1 else ()
        w, grad, total = call(
            scores_kernel,
            [
                out((seqlen, SIDE * count), BF),
                out((seqlen, width), F32 if s == 0 else BF),
                out((8, seqlen), F32),
            ],
            q,
            *negs,
            *others,
            flops=4 * seqlen * SIDE * count * width,
            after=sums[:1],
            name="scores",
        )
        weights.append(w)
        sums.append(grad)
        totals.append(total)
    sums[1:] = across(sums[1:], "queries")
    pack = totals[-1]
    packs = [pack] + across([pack] * 3, "queries")
    pre, mixed, output = call(
        again_kernel,
        [
            out((seqlen, 4 * width), F32),
            out((seqlen, width), F32),
            out((seqlen, width), F32),
        ],
        seq_len,
        history,
        in_weight,
        out_weight,
        smem=(0,),
        flops=2 * seqlen * width * 6 * width,
        after=(pack,),
        name="layer_again",
    )
    half = out((count, width // 2), BF)
    pair = out((2, count, width // 2), BF)
    own_sum, first, second, third, last, loss, factor = call(
        neg_kernel,
        [out((count, width), F32), pair, pair, half, half, out((1, 1), F32), out((seqlen, 1), F32)],
        seq_len,
        *packs,
        *queries,
        *weights,
        smem=(0,),
        flops=2 * SIDE * seqlen * SIDE * count * width,
        after=(output,),
        name="negative_sums",
    )
    row_grad, keep, send = call(
        backward_kernel,
        [
            out((seqlen, width), BF),
            out((width // 2, 5 * width), BF),
            out((width // 2, 5 * width), BF),
        ],
        seq_len,
        at,
        factor,
        *sums,
        history,
        pre,
        mixed,
        output,
        in_weight,
        out_weight,
        smem=(0, 1),
        scratch=[
            pltpu.VMEM((seqlen, width), BF),
            pltpu.VMEM((seqlen, width), BF),
            pltpu.VMEM((seqlen, 4 * width), BF),
        ],
        flops=2 * seqlen * width * 14 * width,
        name="backward",
    )
    got = shift_by(send, "core", 1)
    z_parts = exchanged(scatter(at, 2, [keep, got]), "z")
    (going,) = call(
        going_kernel,
        [out((devices * SLOTS, width), BF)],
        slots,
        row_grad,
        flops=2 * devices * SLOTS * seqlen * width,
        name="going",
    )
    arrived = lax.all_to_all(
        going.reshape(devices, SLOTS, width), AXES, split_axis=0, concat_axis=0, tiled=True
    ).reshape(devices * SLOTS, width)
    first, second = square(first, "x"), square(second, "y")
    third, last = call(turn_kernel, [half, half], third, first, last, second, name="turn")
    third, last = square(third, "y"), square(last, "x")
    y_first = scatter(at, 1, z_parts, (first, second))
    piece = reduced(y_first, (third, last, arrived))
    table_grad, table_done = table_grad_of(
        asked.reshape(1, devices * SLOTS), arrived, neg_rows, own_rows, (own_sum, first, second, third, last), owned
    )
    in_grad, out_grad = gathered(at, piece, (table_done,))
    return (loss.reshape(1), in_grad, out_grad, table_grad)


def solution(mesh):
    return jax.shard_map(
        local,
        mesh=mesh,
        in_specs=(
            P(AXES, None),
            P(AXES, None, None),
            P(AXES),
            P(AXES, None),
            P("group", "member"),
            P(),
            P(),
        ),
        out_specs=(P(AXES), P(), P(), P(AXES, None)),
        check_vma=False,
    )
```

```python
import functools
import jax
import jax.numpy as jnp
from jax import lax
from jax.experimental import pallas as pl
from jax.experimental.pallas import tpu as pltpu
from jax.sharding import PartitionSpec as P

HEADS = 4
SLOTS = 8
SIDE = 4
TEMP = 20.0
BF = jnp.bfloat16
F32 = jnp.float32
AXES = ("group", "member")
MIB = 1024 * 1024


def mm(a, b):
    return jnp.dot(a, b, preferred_element_type=F32)


def mm_nt(a, b):
    return lax.dot_general(a, b, (((1,), (1,)), ((), ())), preferred_element_type=F32)


def mm_tn(a, b):
    return lax.dot_general(a, b, (((0,), (0,)), ((), ())), preferred_element_type=F32)


def iota(shape, dim):
    return lax.broadcasted_iota(jnp.int32, shape, dim)


def ones_where(mask):
    return jnp.where(mask, 1.0, 0.0).astype(BF)


def sigmoid(v):
    return 0.5 * jnp.tanh(0.5 * v) + 0.5


def norm_parts(values):
    centered = values - jnp.mean(values, axis=-1, keepdims=True)
    scale = lax.rsqrt(jnp.mean(centered * centered, axis=-1, keepdims=True) + 1e-05)
    return centered * scale, scale


def norm_back(unit, scale, grad):
    return scale * (
        grad
        - jnp.mean(grad, axis=-1, keepdims=True)
        - unit * jnp.mean(grad * unit, axis=-1, keepdims=True)
    )


def row_to_col(row):
    size = row.shape[1]
    eye = iota((128, 128), 0) == iota((128, 128), 1)
    parts = [
        jnp.sum(jnp.where(eye, row[:, k : k + 128], 0), axis=1, keepdims=True)
        for k in range(0, size, 128)
    ]
    return jnp.concatenate(parts, axis=0)


def col_to_rows(col):
    return jnp.transpose(jnp.broadcast_to(col, (col.shape[0], 128)))[:8]


class Fetched:
    def __init__(self, source, here, sem):
        self.here, self.shape, self.waited = here, here.shape, False
        self.copy = pltpu.make_async_copy(source, here, sem)
        self.copy.start()

    def __getitem__(self, index):
        if not self.waited:
            self.copy.wait()
            self.waited = True
        return self.here[index]


class Sent:
    def __init__(self, target, here, sems):
        self.target, self.here, self.sems, self.copies = target, here, sems, []
        self.shape, self.dtype = here.shape, here.dtype

    def __getitem__(self, index):
        return self.here[index]

    def __setitem__(self, index, value):
        self.here[index] = value
        if index is Ellipsis:
            source, target = self.here, self.target
        else:
            source, target = self.here.at[index], self.target.at[index]
        copy = pltpu.make_async_copy(source, target, self.sems.at[len(self.copies)])
        copy.start()
        self.copies.append(copy)


PARTS = 8
FAR = False


def call(
    kernel, outs, *args, smem=(), far=(), far_out=(), flops=0, name=None, scratch=(), after=(), vmem=40
):
    if not FAR:
        far, far_out = (), ()
    in_specs = [
        pl.BlockSpec(memory_space=pltpu.SMEM if i in smem else pl.ANY if i in far else pltpu.VMEM)
        for i in range(len(args))
    ] + [pl.BlockSpec(memory_space=pl.ANY)] * len(after)
    given, late, shown = len(args), len(after), len(outs)
    hidden = [pltpu.VMEM(args[i].shape, args[i].dtype) for i in far]
    hidden += [pltpu.VMEM(outs[i].shape, outs[i].dtype) for i in far_out]
    hidden += [pltpu.SemaphoreType.DMA((len(far) + 1,))]
    hidden += [pltpu.SemaphoreType.DMA((PARTS,)) for _ in far_out]

    def body(*refs):
        ins, results = list(refs[:given]), list(refs[given + late : given + late + shown])
        rest = refs[given + late + shown :]
        own, rest = rest[: len(scratch)], rest[len(scratch) :]
        sems = rest[len(far) + len(far_out)]
        for n, i in enumerate(far):
            ins[i] = Fetched(ins[i], rest[n], sems.at[n])
        sent = []
        for n, i in enumerate(far_out):
            results[i] = Sent(results[i], rest[len(far) + n], rest[len(far) + len(far_out) + 1 + n])
            sent.append(results[i])
        kernel(*ins, *results, *own)
        for result in sent:
            for copy in result.copies:
                copy.wait()

    moved = sum(a.size * a.dtype.itemsize for a in args)
    moved += sum(o.size * o.dtype.itemsize for o in outs)
    return pl.pallas_call(
        body,
        out_shape=outs,
        in_specs=in_specs,
        out_specs=[
            pl.BlockSpec(memory_space=pltpu.HBM if i in far_out else pltpu.VMEM)
            for i in range(len(outs))
        ],
        scratch_shapes=list(scratch) + hidden,
        compiler_params=pltpu.CompilerParams(vmem_limit_bytes=vmem * MIB),
        cost_estimate=pl.CostEstimate(flops=flops, bytes_accessed=moved, transcendentals=0),
        name=name,
    )(*args, *after)


def out(shape, dtype):
    return jax.ShapeDtypeStruct(shape, dtype)


def later(values, after):
    count = len(values)
    anywhere = pl.BlockSpec(memory_space=pl.ANY)
    return pl.pallas_call(
        lambda *refs: None,
        out_shape=[out(v.shape, v.dtype) for v in values],
        in_specs=[anywhere] * (count + len(after)),
        out_specs=[anywhere] * count,
        input_output_aliases={i: i for i in range(count)},
        cost_estimate=pl.CostEstimate(flops=0, bytes_accessed=0, transcendentals=0),
        name="later",
    )(*values, *after)


def slots_kernel(owner_ref, row_ref, slots_ref, req_ref):
    owner = row_to_col(owner_ref[...])
    seqlen = owner.shape[0]
    devices = req_ref.shape[0]
    named = ones_where(owner == iota((seqlen, devices), 1))
    earlier = ones_where(iota((seqlen, seqlen), 0) > iota((seqlen, seqlen), 1))
    before = mm(earlier, named)
    place = jnp.sum(before * named.astype(F32), axis=1, keepdims=True).astype(jnp.int32)
    slots_ref[...] = owner * SLOTS + place
    wanted = row_to_col(row_ref[...])
    at_place = iota((seqlen, 128), 1) == place
    high = jnp.where(at_place, wanted >> 6, 0).astype(F32).astype(BF)
    low = jnp.where(at_place, wanted & 63, 0).astype(F32).astype(BF)
    asked = mm_tn(named, high) * 64.0 + mm_tn(named, low)
    req_ref[...] = asked[:, :SLOTS].astype(jnp.int32)


def find_kernel(asked_ref, table_ref, found_ref):
    asked = asked_ref[...]
    devices = asked.shape[0]
    rows = table_ref.shape[0]
    block = 256
    high = (asked >> 6).astype(F32).astype(BF)
    low = (asked & 63).astype(F32).astype(BF)
    for k in range(0, devices * SLOTS, block):
        spread = ones_where(
            (iota((block, devices), 0) + k) // SLOTS == iota((block, devices), 1)
        )
        every = mm(spread, high) * 64.0 + mm(spread, low)
        mine = (iota((block, SLOTS), 0) & (SLOTS - 1)) == iota((block, SLOTS), 1)
        ids = jnp.sum(jnp.where(mine, every, 0.0), axis=1, keepdims=True).astype(jnp.int32)
        pick = ones_where(ids == iota((block, rows), 1))
        found_ref[k : k + block, :] = mm(pick, table_ref[...]).astype(BF)


def own_kernel(ids_ref, table_ref, rows_ref, unit_ref):
    ids = row_to_col(ids_ref[...])
    rows = table_ref.shape[0]
    block = 256
    for k in range(0, ids.shape[0], block):
        pick = ones_where(ids[k : k + block] == iota((block, rows), 1))
        got = mm(pick, table_ref[...])
        rows_ref[k : k + block, :] = got.astype(BF)
        scale = lax.rsqrt(jnp.sum(got * got, axis=-1, keepdims=True) + 1e-06)
        unit_ref[k : k + block, :] = (got * scale).astype(BF)


def attention_of(query, key, length):
    seqlen, head_size = query.shape
    scores = mm_nt(query, key) * head_size ** (-0.5)
    at, of = iota((seqlen, seqlen), 0), iota((seqlen, seqlen), 1)
    allowed = (of <= at) & (of < length)
    share = jnp.where(allowed, 1.0 / length.astype(F32), 0.0)
    return scores, share


def following_of(history):
    seqlen = history.shape[0]
    moved = pltpu.roll(history, seqlen - 1, 0)
    return jnp.where(iota(history.shape, 0) < seqlen - 1, moved, 0.0)


def layer(length, history, in_ref, out_ref, mixed_ref, pre_ref=None):
    width = history.shape[1]
    head = width // HEADS
    normed = norm_parts(history.astype(F32))[0].astype(BF)
    parts = []
    for k in range(4):
        pre = mm(normed, in_ref[:, k * width : (k + 1) * width])
        if pre_ref is not None:
            pre_ref[:, k * width : (k + 1) * width] = pre
        parts.append((pre * sigmoid(pre)).astype(BF))
    gate, values, queries, keys = parts
    for h in range(HEADS):
        cols = slice(h * head, (h + 1) * head)
        scores, share = attention_of(queries[:, cols], keys[:, cols], length)
        attention = (scores * sigmoid(scores) * share).astype(BF)
        mixed_ref[:, cols] = mm(attention, values[:, cols])
    gated = (norm_parts(mixed_ref[...])[0] * gate.astype(F32)).astype(BF)
    return mm(gated, out_ref[...]) + history.astype(F32)


def forward_kernel(
    len_ref, back_ref, slots_ref, in_ref, out_ref, hist_ref, query_ref, pos_ref, mixed_ref
):
    seqlen = hist_ref.shape[0]
    length = len_ref[0]
    pick = ones_where(slots_ref[...] == iota((seqlen, back_ref.shape[0]), 1))
    hist_ref[...] = mm(pick, back_ref[...]).astype(BF)
    output = layer(length, hist_ref[...], in_ref, out_ref, mixed_ref)
    scale = lax.rsqrt(jnp.sum(output * output, axis=-1, keepdims=True) + 1e-06)
    query_unit = output * scale
    query_ref[...] = query_unit.astype(BF)
    following = following_of(hist_ref[...].astype(F32))
    pos_scale = lax.rsqrt(jnp.sum(following * following, axis=-1, keepdims=True) + 1e-06)
    pos_score = TEMP * jnp.sum(query_unit * (following * pos_scale), axis=-1, keepdims=True)
    rows = col_to_rows(pos_score)
    usable = jnp.where(iota(rows.shape, 1) < length - 1, 1.0, 0.0)
    pos_ref[...] = jnp.where(iota(rows.shape, 0) == 0, rows, usable)


def again_kernel(
    len_ref, hist_ref, in_ref, out_ref, pre_ref, mixed_ref, output_ref
):
    output_ref[...] = layer(len_ref[0], hist_ref[...], in_ref, out_ref, mixed_ref, pre_ref)


def scores_kernel(query_ref, *refs):
    negs, others, (weights_ref, grad_ref, total_ref) = refs[:SIDE], refs[SIDE:-3], refs[-3:]
    query = query_ref[...]
    total = jnp.zeros((query.shape[0], 1), F32)
    grad = jnp.zeros(query.shape, F32)
    for k, neg_ref in enumerate(negs):
        neg = neg_ref[...]
        size = neg.shape[0]
        weight = jnp.exp(TEMP * mm_nt(query, neg))
        total = total + jnp.sum(weight, axis=1, keepdims=True)
        weight = weight.astype(BF)
        weights_ref[:, k * size : (k + 1) * size] = weight
        grad = grad + mm(weight, neg)
    grad_ref[...] = grad.astype(grad_ref.dtype)
    total = col_to_rows(total)
    row = iota(total.shape, 0)
    for k, ref in enumerate(others[:-1]):
        total = jnp.where(row == k, ref[...], total)
    if others:
        total = jnp.where(row == SIDE, others[-1][0:1, :], total)
        total = jnp.where(row == SIDE + 1, others[-1][1:2, :], total)
    total_ref[...] = total


def row_to_f32_col(row):
    return jnp.transpose(jnp.broadcast_to(row, (128, row.shape[1])))[:, 0:1]


def neg_kernel(len_ref, *refs):
    packs, queries, weights = refs[:SIDE], refs[SIDE : 2 * SIDE], refs[2 * SIDE : 3 * SIDE]
    own_ref, first_ref, second_ref, third_ref, last_ref, loss_ref, factor_ref = refs[3 * SIDE :]
    half = own_ref.shape[1] // 2
    scaled = []
    for k, query_ref in enumerate(queries):
        pos_score, usable = packs[k][SIDE : SIDE + 1, :], packs[k][SIDE + 1 : SIDE + 2, :]
        total = jnp.exp(pos_score)
        for j, ref in enumerate(packs):
            total = total + ref[j ^ k : (j ^ k) + 1, :]
        log_total = jnp.log(total)
        if k == 0:
            loss = jnp.sum((log_total - pos_score) * usable, axis=1, keepdims=True)
            loss_ref[...] = loss / (len_ref[0] - 1).astype(F32)
        factor = row_to_f32_col(TEMP * usable * jnp.exp(-log_total))
        if k == 0:
            factor_ref[...] = factor
        scaled.append((query_ref[...].astype(F32) * factor).astype(BF))
    for k in range(SIDE):
        size = own_ref.shape[0]
        cols = slice(k * size, (k + 1) * size)
        total = mm_tn(weights[0][:, cols], scaled[0])
        for w, q in zip(weights[1:], scaled[1:]):
            total = total + mm_tn(w[:, cols], q)
        left, right = total[:, :half].astype(BF), total[:, half:].astype(BF)
        if k == 0:
            own_ref[...] = total
        elif k == 1:
            first_ref[0], last_ref[...] = left, right
        elif k == 2:
            third_ref[...], second_ref[0] = left, right
        else:
            first_ref[1], second_ref[1] = left, right


def turn_kernel(third_ref, from_first, last_ref, from_second, over_third, over_last):
    third = third_ref[...].astype(F32) + from_first[1].astype(F32)
    over_third[...] = third.astype(BF)
    last = last_ref[...].astype(F32) + from_second[1].astype(F32)
    over_last[...] = last.astype(BF)


def backward_kernel(
    len_ref, at_ref, factor_ref, sum0, sum1, sum2, sum3, hist_ref, pre_ref, mixed_ref, output_ref,
    in_ref, out_ref, slots_ref,
    going_ref, keep_ref, send_ref,
    normed_ref, gated_ref, dpre_ref, row_ref,
):
    length = len_ref[0]
    core = at_ref[3]
    seqlen, width = hist_ref.shape
    head = width // HEADS
    history = hist_ref[...].astype(F32)
    output = output_ref[...]
    query_scale = lax.rsqrt(jnp.sum(output * output, axis=-1, keepdims=True) + 1e-06)
    query_unit = output * query_scale
    following = following_of(history)
    pos_scale = lax.rsqrt(jnp.sum(following * following, axis=-1, keepdims=True) + 1e-06)
    pos_unit = following * pos_scale
    pos_score = TEMP * jnp.sum(query_unit * pos_unit, axis=-1, keepdims=True)
    from_negs = jnp.zeros((seqlen, width), F32)
    for ref in (sum0, sum1, sum2, sum3):
        from_negs = from_negs + ref[...].astype(F32)
    usable = jnp.where(iota((seqlen, 1), 0) < length - 1, 1.0, 0.0)
    factor = factor_ref[...]
    pos_grad = factor * jnp.exp(pos_score) - TEMP * usable
    query_grad = pos_grad * pos_unit + factor * from_negs
    output_grad = query_scale * (
        query_grad - query_unit * jnp.sum(query_unit * query_grad, axis=-1, keepdims=True)
    )
    unit_grad = pos_grad * query_unit
    next_grad = pos_scale * (
        unit_grad - pos_unit * jnp.sum(pos_unit * unit_grad, axis=-1, keepdims=True)
    )
    shifted = jnp.where(iota((seqlen, width), 0) > 0, pltpu.roll(next_grad, 1, 0), 0.0)

    def hidden_of(k):
        pre = pre_ref[:, k * width : (k + 1) * width]
        return (pre * sigmoid(pre)).astype(BF)

    def store(k, cols, grad):
        cols = slice(k * width + cols.start, k * width + cols.stop)
        pre = pre_ref[:, cols]
        s = sigmoid(pre)
        grad = grad.astype(BF).astype(F32) * (s * (1.0 + pre * (1.0 - s)))
        dpre_ref[:, cols] = grad.astype(BF)

    gate = hidden_of(0).astype(F32)
    mixed_unit, mixed_scale = norm_parts(mixed_ref[...])
    gated_ref[...] = (mixed_unit * gate).astype(BF)
    output_bf = output_grad.astype(BF)
    d_gated = mm_nt(output_bf, out_ref[...]).astype(BF).astype(F32)
    store(0, slice(0, width), d_gated * mixed_unit)
    d_mixed = norm_back(mixed_unit, mixed_scale, d_gated * gate).astype(BF)
    values, queries, keys = hidden_of(1), hidden_of(2), hidden_of(3)
    for h in range(HEADS):
        cols = slice(h * head, (h + 1) * head)
        q, k, v, d = queries[:, cols], keys[:, cols], values[:, cols], d_mixed[:, cols]
        scores, share = attention_of(q, k, length)
        s = sigmoid(scores)
        attention = (scores * s * share).astype(BF)
        d_attention = mm_nt(d, v).astype(BF).astype(F32)
        d_scores = d_attention * share * (s * (1.0 + scores * (1.0 - s)))
        d_scores = (d_scores * head ** (-0.5)).astype(BF)
        store(1, cols, mm_tn(attention, d))
        store(2, cols, mm(d_scores, k))
        store(3, cols, mm_tn(d_scores, q))
    normed, scale = norm_parts(history)
    normed_ref[...] = normed.astype(BF)
    half = width // 2
    for ref, which in ((send_ref, 1 - core), (keep_ref, core)):
        rows = pl.ds(pl.multiple_of(which * half, half), half)
        mine = normed_ref[:, rows]
        for k in range(4):
            cols = slice(k * width, (k + 1) * width)
            ref[:, cols] = mm_tn(mine, dpre_ref[:, cols]).astype(BF)
        ref[:, 4 * width :] = mm_tn(gated_ref[:, rows], output_bf).astype(BF)
    d_normed = mm_nt(dpre_ref[...], in_ref[...]).astype(BF).astype(F32)
    row_ref[...] = (output_grad + norm_back(normed, scale, d_normed) + shifted).astype(BF)
    pick = ones_where(slots_ref[...] == iota((seqlen, going_ref.shape[0]), 1))
    going_ref[...] = mm_tn(pick, row_ref[...]).astype(BF)


def table_kernel(
    asked_ref, arrived_ref, ids_ref, rows_ref, own_ref, first_ref, second_ref, third_ref, last_ref,
    table_ref, done_ref, grad_ref,
):
    block = table_ref.shape[0]

    @pl.when(pl.program_id(0) == 0)
    def _():
        rows = rows_ref[...].astype(F32)
        scale = lax.rsqrt(jnp.sum(rows * rows, axis=-1, keepdims=True) + 1e-06)
        unit = rows * scale
        left = first_ref[0].astype(F32) + third_ref[...].astype(F32)
        right = second_ref[0].astype(F32) + last_ref[...].astype(F32)
        total = own_ref[...] + jnp.concatenate([left, right], axis=1)
        grad = scale * (total - unit * jnp.sum(unit * total, axis=-1, keepdims=True))
        grad_ref[...] = grad.astype(BF)
        done_ref[...] = jnp.zeros(done_ref.shape, F32)

    first = pl.program_id(0) * block
    asked, ids = asked_ref[...], ids_ref[...]
    pick = ones_where(asked == iota((block, asked.shape[1]), 0) + first)
    total = mm(pick, arrived_ref[...])
    pick = ones_where(ids == iota((block, ids.shape[1]), 0) + first)
    table_ref[...] = total + mm(pick, grad_ref[...])


def table_grad_of(asked, arrived, ids, rows, negs, owned):
    width = arrived.shape[1]
    block = 512
    whole = pl.BlockSpec(memory_space=pltpu.VMEM)
    return pl.pallas_call(
        table_kernel,
        grid=(owned // block,),
        out_shape=[out((owned, width), F32), out((8, 128), F32)],
        in_specs=[whole] * 9,
        out_specs=[
            pl.BlockSpec((block, width), lambda i: (i, 0)),
            pl.BlockSpec((8, 128), lambda i: (0, 0)),
        ],
        scratch_shapes=[pltpu.VMEM(rows.shape, BF)],
        compiler_params=pltpu.CompilerParams(vmem_limit_bytes=40 * MIB),
        cost_estimate=pl.CostEstimate(
            flops=2 * owned * (arrived.shape[0] + rows.shape[0]) * width,
            bytes_accessed=owned * width * 4,
            transcendentals=0,
        ),
        name="table_grad",
    )(asked, arrived, ids, rows, *negs)


def quarters(at_ref, place, total_ref, outs):
    me = at_ref[place]
    for s, ref in enumerate(outs):
        size = ref.shape[0]
        which = (me + s) & (SIDE - 1)
        part = total_ref[pl.ds(pl.multiple_of(which * size, size), size), :]
        ref[...] = part.astype(ref.dtype)


def sum_of(refs):
    total = refs[0][...].astype(F32)
    for ref in refs[1:]:
        total = total + ref[...].astype(F32)
    return total


def scatter_kernel(place, count, at_ref, *refs):
    ins, outs, total_ref = refs[:count], refs[count:-1], refs[-1]
    total_ref[...] = sum_of(ins)
    quarters(at_ref, place, total_ref, outs)


def last_kernel(*refs):
    refs[-1][...] = sum_of(refs[:-1]).astype(refs[-1].dtype)


def total_kernel(p0, p1, p2, p3, total_ref):
    even = p0[...].astype(F32) + p2[...].astype(F32)
    odd = p1[...].astype(F32) + p3[...].astype(F32)
    total_ref[...] = (even + odd).astype(total_ref.dtype)


def stack_kernel(*refs):
    size = refs[0].shape[0]
    for k, ref in enumerate(refs[:-1]):
        refs[-1][k * size : (k + 1) * size] = ref[...]


def place_kernel(at_ref, mine_ref, other_ref, in_ref, out_ref):
    y, z, core = at_ref[1], at_ref[2], at_ref[3]
    count, rows, cols = mine_ref.shape
    half, width = in_ref.shape[0] // 2, in_ref.shape[1]
    for which, ref in ((core, mine_ref), (1 - core, other_ref)):
        for i in range(count):
            row = which * half + ((z - i // SIDE) & 3) * (half // SIDE)
            row = row + ((y - i % SIDE) & 3) * rows
            place = pl.ds(pl.multiple_of(row, rows), rows)
            part = ref[i].astype(F32)
            in_ref[place, :] = part[:, :width]
            out_ref[place, :] = part[:, width:]


def moves(axis, shift):
    if axis == "z":
        return "group", [(z * 2 + c, (z + shift) % SIDE * 2 + c) for z in range(SIDE) for c in range(2)]
    if axis == "core":
        return "group", [(g, g ^ 1) for g in range(2 * SIDE)]
    pairs = [(y, x) for y in range(SIDE) for x in range(SIDE)]
    if axis == "x":
        return "member", [(y * SIDE + x, y * SIDE + (x + shift) % SIDE) for y, x in pairs]
    return "member", [(y * SIDE + x, (y + shift) % SIDE * SIDE + x) for y, x in pairs]


def shift_by(value, axis, shift):
    name, pairs = moves(axis, shift)
    return lax.ppermute(value, name, pairs)


def spread(value, axis):
    return [value] + [shift_by(value, axis, s) for s in range(1, SIDE)]


def square(value, axis):
    step = 3 if axis == "x" else 3 * SIDE
    return lax.ppermute(value, "member", [(m, m ^ step) for m in range(SIDE * SIDE)])


def across(value, kind):
    step = 1 if kind == "queries" else 3
    masks = (step, step * SIDE, step * SIDE + step)
    return [
        lax.ppermute(v, "member", [(m, m ^ mask) for m in range(SIDE * SIDE)])
        for v, mask in zip(value, masks)
        if v is not None
    ]


def scatter(at, place, ins, after=()):
    rows, cols = ins[0].shape
    piece = (rows // SIDE, cols)
    return call(
        functools.partial(scatter_kernel, place, len(ins)),
        [out(piece, F32)] + [out(piece, BF)] * (SIDE - 1),
        at,
        *ins,
        smem=(0,),
        scratch=[pltpu.VMEM((rows, cols), F32)],
        after=after,
        name="scatter",
    )


def exchanged(parts, axis):
    return [parts[0]] + [shift_by(parts[s], axis, s) for s in range(1, SIDE)]


def reduced(parts, after):
    (piece,) = call(last_kernel, [out(parts[0].shape, BF)], *exchanged(parts, "y"), name="last")
    (piece,) = call(
        total_kernel, [out(piece.shape, BF)], *spread(piece, "x"), after=after, name="total"
    )
    return piece


def gathered(at, piece, after):
    rows, cols = piece.shape
    width = rows * 2 * SIDE * SIDE
    piece = jnp.concatenate(spread(piece[None], "y"), axis=0)
    (piece,) = call(
        stack_kernel,
        [out((SIDE * SIDE, rows, cols), BF)],
        *spread(piece, "z"),
        after=after,
        name="stack",
    )
    return call(
        place_kernel,
        [out((width, cols - width), F32), out((width, width), F32)],
        at,
        piece,
        shift_by(piece, "core", 1),
        smem=(0,),
        name="place",
    )


def local(hist_row, hist_owner, seq_len, item_table, neg_rows, in_weight, out_weight):
    devices = lax.axis_size(AXES)
    seqlen = hist_row.shape[1]
    owned, width = item_table.shape
    count = neg_rows.shape[1]
    group, member = lax.axis_index("group"), lax.axis_index("member")
    at = jnp.stack([member % SIDE, member // SIDE, group // 2, group % 2]).astype(jnp.int32)

    own_rows, own_bf = call(
        own_kernel,
        [out((count, width), BF), out((count, width), BF)],
        neg_rows,
        item_table,
        flops=2 * count * owned * width,
        name="own_negatives",
    )
    negs = [own_bf] + across([own_bf] * 3, "negatives")
    slots, requests = call(
        slots_kernel,
        [out((seqlen, 1), jnp.int32), out((devices, SLOTS), jnp.int32)],
        hist_owner.reshape(1, seqlen),
        hist_row,
        after=(own_bf,),
        name="slots",
    )
    asked = lax.all_to_all(requests, AXES, split_axis=0, concat_axis=0, tiled=True)
    (found,) = call(
        find_kernel,
        [out((devices * SLOTS, width), BF)],
        asked,
        item_table,
        flops=2 * devices * SLOTS * owned * width,
        after=(negs[1], negs[2]),
        name="find_rows",
    )
    back = lax.all_to_all(
        found.reshape(devices, SLOTS, width), AXES, split_axis=0, concat_axis=0, tiled=True
    ).reshape(devices * SLOTS, width)
    history, query, pos = call(
        forward_kernel,
        [out((seqlen, width), BF), out((seqlen, width), BF), out((8, seqlen), F32)],
        seq_len,
        back,
        slots,
        in_weight,
        out_weight,
        smem=(0,),
        scratch=[pltpu.VMEM((seqlen, width), F32)],
        flops=2 * seqlen * width * (devices * SLOTS + 6 * width),
        name="forward",
    )
    queries = [query] + across([query] * 3, "queries")
    weights, sums, totals = [], [], []
    for s, q in enumerate(queries):
        others = (*totals, pos) if s == SIDE - 1 else ()
        w, grad, total = call(
            scores_kernel,
            [
                out((seqlen, SIDE * count), BF),
                out((seqlen, width), F32 if s == 0 else BF),
                out((8, seqlen), F32),
            ],
            q,
            *negs,
            *others,
            flops=4 * seqlen * SIDE * count * width,
            after=sums[:1],
            name="scores",
        )
        weights.append(w)
        sums.append(grad)
        totals.append(total)
    sums[1:] = across(sums[1:], "queries")
    pack = totals[-1]
    packs = [pack] + across([pack] * 3, "queries")
    pre, mixed, output = call(
        again_kernel,
        [
            out((seqlen, 4 * width), F32),
            out((seqlen, width), F32),
            out((seqlen, width), F32),
        ],
        seq_len,
        history,
        in_weight,
        out_weight,
        smem=(0,),
        flops=2 * seqlen * width * 6 * width,
        after=(pack,),
        name="layer_again",
    )
    half = out((count, width // 2), BF)
    pair = out((2, count, width // 2), BF)
    own_sum, first, second, third, last, loss, factor = call(
        neg_kernel,
        [out((count, width), F32), pair, pair, half, half, out((1, 1), F32), out((seqlen, 1), F32)],
        seq_len,
        *packs,
        *queries,
        *weights,
        smem=(0,),
        flops=2 * SIDE * seqlen * SIDE * count * width,
        after=(output,),
        name="negative_sums",
    )
    going, keep, send = call(
        backward_kernel,
        [
            out((devices * SLOTS, width), BF),
            out((width // 2, 5 * width), BF),
            out((width // 2, 5 * width), BF),
        ],
        seq_len,
        at,
        factor,
        *sums,
        history,
        pre,
        mixed,
        output,
        in_weight,
        out_weight,
        slots,
        smem=(0, 1),
        scratch=[
            pltpu.VMEM((seqlen, width), BF),
            pltpu.VMEM((seqlen, width), BF),
            pltpu.VMEM((seqlen, 4 * width), BF),
            pltpu.VMEM((seqlen, width), BF),
        ],
        flops=2 * seqlen * width * 14 * width,
        name="backward",
    )
    got = shift_by(send, "core", 1)
    z_parts = exchanged(scatter(at, 2, [keep, got]), "z")
    arrived = lax.all_to_all(
        going.reshape(devices, SLOTS, width), AXES, split_axis=0, concat_axis=0, tiled=True
    ).reshape(devices * SLOTS, width)
    first, second = square(first, "x"), square(second, "y")
    third, last = call(turn_kernel, [half, half], third, first, last, second, name="turn")
    third, last = square(third, "y"), square(last, "x")
    y_first = scatter(at, 1, z_parts, (first, second))
    piece = reduced(y_first, (third, last, arrived))
    table_grad, table_done = table_grad_of(
        asked.reshape(1, devices * SLOTS), arrived, neg_rows, own_rows, (own_sum, first, second, third, last), owned
    )
    in_grad, out_grad = gathered(at, piece, (table_done,))
    return (loss.reshape(1), in_grad, out_grad, table_grad)


def solution(mesh):
    return jax.shard_map(
        local,
        mesh=mesh,
        in_specs=(
            P(AXES, None),
            P(AXES, None, None),
            P(AXES),
            P(AXES, None),
            P("group", "member"),
            P(),
            P(),
        ),
        out_specs=(P(AXES), P(), P(), P(AXES, None)),
        check_vma=False,
    )
```
